32 devices in a mesh: space: 8 (over z, x), blk: 4 (over y, core).
Axes of the slice: x: 2, y: 2, z: 4, core: 2. Of those that a mesh axis runs over, the one named last changes fastest.
Arguments:
- snapshots: float32 [64, 16, 16, 512], P('space', None, None, 'blk'), may hold values from -40 to 40, as said below
Outputs:
- rotated: float32 [64, 16, 16, 512], P('space', None, None, 'blk')
The draws below stay inside these ranges and needn't reach their ends.
Inputs may be any that keep to these rules, and one draw needn't show every extreme that they name: `snapshots`: snapshot values are finite reals.
All inputs are finite; a program needn't handle non-finite values.
Results may differ from the reference program's by a relative error of at most 0.0003.
Values sent between devices are 32-bit elements; how exact they have to be, the bound alone decides.
No kernel may reach another device: no remote copies, remote signals or barrier semaphores. Data moves between devices by JAX's collectives and lax.ppermute only.
A program may use at most 64 MiB of HBM per device.

```python
import jax
import jax.numpy as jnp
from jax import lax

GY = 16
GZ = 16
BLOCK = 128
ROUNDS = 2
NX = 64
SNAPS = 512
N_BLK = 4


def draw_snapshots(key, part):
    key_noise, key_class, key_shared, key_amp = jax.random.split(key, 4)
    shape = (NX, GY, GZ, SNAPS)
    classes = 8
    noise = jax.random.truncated_normal(key_noise, -4.0, 4.0, shape, jnp.float32)
    amps = jax.random.uniform(key_amp, (SNAPS,), jnp.float32, 0.5, 1.5)
    labels = jax.random.randint(key_class, (SNAPS,), 0, classes)
    shared = jax.random.truncated_normal(key_shared, -4.0, 4.0, (NX, GY, GZ, classes), jnp.float32)
    picked = jnp.take(shared, labels, axis=3)
    return (noise + amps * picked).astype(jnp.float32)


def setup_inputs(seed: int = 0) -> dict:
    key_of = jax.random.split(jax.random.key(seed), 2)
    return {
        "snapshots": draw_snapshots(jax.random.fold_in(key_of[1], 71), 0),
    }


def degree_field(size_x, size_y, size_z):
    pos_x = jnp.arange(size_x, dtype=jnp.int32)
    pos_y = jnp.arange(size_y, dtype=jnp.int32)
    pos_z = jnp.arange(size_z, dtype=jnp.int32)
    deg_x = (pos_x > 0).astype(jnp.float32) + (pos_x < size_x - 1).astype(jnp.float32)
    deg_y = (pos_y > 0).astype(jnp.float32) + (pos_y < size_y - 1).astype(jnp.float32)
    deg_z = (pos_z > 0).astype(jnp.float32) + (pos_z < size_z - 1).astype(jnp.float32)
    return deg_x[:, None, None] + deg_y[None, :, None] + deg_z[None, None, :]

def weighted(block, degree):
    padded = jnp.pad(block, ((1, 1), (1, 1), (1, 1), (0, 0)))
    near = padded[2:, 1:-1, 1:-1] + padded[:-2, 1:-1, 1:-1]
    near = near + padded[1:-1, 2:, 1:-1] + padded[1:-1, :-2, 1:-1]
    near = near + padded[1:-1, 1:-1, 2:] + padded[1:-1, 1:-1, :-2]
    return block + (degree[..., None] * block - near)

def gram_of(left, right):
    width = left.shape[-1]
    return lax.dot_general(left.reshape(-1, width).astype(jnp.float32), right.reshape(-1, width).astype(jnp.float32), (((0,), (0,)), ((), ())), precision=lax.Precision.HIGHEST, preferred_element_type=jnp.float32)

def rotation(own_diag, peer_diag, cross, parity):
    denom = jnp.diagonal(own_diag)[:, None] + jnp.diagonal(peer_diag)[None, :]
    ratios = cross / denom
    eye_mat = jnp.eye(cross.shape[0], dtype=jnp.float32)
    normal_mat = eye_mat + jnp.dot(ratios.astype(jnp.float32), ratios.T.astype(jnp.float32), precision=lax.Precision.HIGHEST, preferred_element_type=jnp.float32)
    factor = jnp.linalg.cholesky(normal_mat)
    inverse = jax.scipy.linalg.cho_solve((factor, True), eye_mat)
    solved = jax.scipy.linalg.cho_solve((factor, True), ratios)
    keep_mat = 2.0 * inverse - eye_mat
    take_mat = 2.0 * parity * solved.T
    return (keep_mat, take_mat)

def mix_blocks(own_block, peer_block, keep_mat, take_mat):
    width = own_block.shape[-1]
    first = jnp.dot(own_block.reshape(-1, width).astype(jnp.float32), keep_mat.astype(jnp.float32), precision=lax.Precision.HIGHEST, preferred_element_type=jnp.float32)
    second = jnp.dot(peer_block.reshape(-1, width).astype(jnp.float32), take_mat.astype(jnp.float32), precision=lax.Precision.HIGHEST, preferred_element_type=jnp.float32)
    return (first + second).reshape(own_block.shape)

def reference(snapshots):
    degree = degree_field(NX, GY, GZ)
    field = snapshots
    indices = jnp.arange(N_BLK, dtype=jnp.int32)
    for sweep_round in range(ROUNDS):

        def take_block(which):
            return lax.dynamic_slice_in_dim(field, (which * BLOCK).astype(jnp.int32), BLOCK, 3)

        def stats(which):
            own_block = take_block(which)
            peer_block = take_block(jnp.bitwise_xor(which, 1 << sweep_round))
            image = weighted(own_block, degree)
            return (gram_of(image, own_block), gram_of(image, peer_block))
        diag_all, cross_all = lax.map(stats, indices)

        def update(which):
            partner = jnp.bitwise_xor(which, 1 << sweep_round)
            parity = ((which >> sweep_round & 1) * 2 - 1).astype(jnp.float32)
            keep_mat, take_mat = rotation(diag_all[which], diag_all[partner], cross_all[which], parity)
            return mix_blocks(take_block(which), take_block(partner), keep_mat, take_mat)
        stacked = lax.map(update, indices)
        field = jnp.moveaxis(stacked, 0, 3).reshape(NX, GY, GZ, SNAPS)
    return field
```

```python
import functools

import jax
import jax.numpy as jnp
from jax import lax
from jax.experimental import pallas as pl
from jax.experimental.pallas import tpu as pltpu
from jax.sharding import PartitionSpec as P

F32 = jnp.float32
BF16 = jnp.bfloat16
VMEM = pl.BlockSpec(memory_space=pltpu.VMEM)
PARAMS = pltpu.CompilerParams(vmem_limit_bytes=40 * 2**20)
CLOSE = 5e-4
STEPS = 5
CHUNKS = 1


def place():
    space = lax.axis_index("space")
    size = lax.axis_size("space")
    blk = lax.axis_index("blk")
    odd = space % 2
    has_a = jnp.where(odd == 1, 1, jnp.where(space < size - 1, 1, 0))
    has_b = jnp.where(odd == 1, jnp.where(space < size - 1, 1, 0), jnp.where(space > 0, 1, 0))
    return blk % 2, odd, has_a, has_b, (blk // 2) % 2


def cost(micros):
    return pl.CostEstimate(flops=int(micros * 1e9), bytes_accessed=1, transcendentals=0)


def rows_of(chunks, start, count):
    for chunk in chunks:
        if start < chunk.shape[0]:
            return chunk[start:start + count, :]
        start -= chunk.shape[0]


def shape_of(rows, width):
    return jax.ShapeDtypeStruct((rows, width), F32)


def exchanged(value, axis, mask):
    count = lax.axis_size(axis)
    return lax.ppermute(value, axis, [(i, i ^ mask) for i in range(count)])


def halves(value):
    high = value.astype(BF16)
    return high, (value - high.astype(F32)).astype(BF16)


def gram(left, right):
    def one(a, b):
        return lax.dot_general(a, b, (((0,), (0,)), ((), ())), preferred_element_type=F32)

    left_high, left_low = halves(left)
    right_high, right_low = halves(right)
    return one(left_high, right_high) + (one(left_high, right_low) + one(left_low, right_high))


def thirds(value):
    high = value.astype(BF16)
    rest = value - high.astype(F32)
    middle = rest.astype(BF16)
    return high, middle, (rest - middle.astype(F32)).astype(BF16)


def product(left, right):
    a, b, c = thirds(left)
    x, y, z = thirds(right)

    def pair(one, two, three, four):
        return jnp.dot(
            jnp.concatenate([one, two], axis=1), jnp.concatenate([three, four], axis=0),
            preferred_element_type=F32,
        )

    return pair(a, a, x, y) + (pair(b, a, x, z) + pair(c, b, x, y))


def product_3(left, right):
    left_high, left_low = halves(left)
    right_high, right_low = halves(right)
    deep = jnp.dot(
        jnp.concatenate([left_high, left_low], axis=1),
        jnp.concatenate([right_high, right_high], axis=0),
        preferred_element_type=F32,
    )
    return deep + jnp.dot(left_high, right_low, preferred_element_type=F32)


def product_nt(left, right):
    def one(a, b):
        return lax.dot_general(a, b, (((1,), (1,)), ((), ())), preferred_element_type=F32)

    left_high, left_low = halves(left)
    right_high, right_low = halves(right)
    return one(left_high, right_high) + (one(left_high, right_low) + one(left_low, right_high))


def inner_image(at, i, layers, cells_z):
    v = at(i)
    layer, width = v.shape
    place = lax.broadcasted_iota(jnp.int32, (layer, width), 0) % cells_z
    near = at(min(i + 1, layers - 1)) + at(max(i - 1, 0))
    near = near + jnp.concatenate([v[cells_z:], v[-cells_z:]], axis=0)
    near = near + jnp.concatenate([v[:cells_z], v[:-cells_z]], axis=0)
    near = near + jnp.where(place == cells_z - 1, v, pltpu.roll(v, layer - 1, 0))
    near = near + jnp.where(place == 0, v, pltpu.roll(v, 1, 0))
    return 7.0 * v - near


def inner_kernel(cells_y, cells_z, *refs):
    layer = cells_y * cells_z
    chunks = refs[:CHUNKS]
    p_ref, w_ref, c_ref, d_ref = refs[CHUNKS:]
    layers = p_ref.shape[0] // layer
    width = p_ref.shape[1]
    high = place()[0] == 1
    cross = jnp.zeros((width, width), F32)
    diag = jnp.zeros((8, width), F32)

    def at(j):
        return rows_of(chunks, j * layer, layer)

    for i in range(layers):
        rows = slice(i * layer, (i + 1) * layer)
        v = at(i)
        image = inner_image(at, i, layers, cells_z)
        w_ref[rows, :] = image
        diag += jnp.sum((image * v).reshape(layer // 8, 8, width), axis=0)
        peer = p_ref[rows, :]
        cross += gram(jnp.where(high, peer, image), jnp.where(high, image, peer))
    c_ref[...] = cross
    d_ref[...] = diag


def edge_kernel(edge_a, edge_b, p_ref, c_ref, d_ref, near_a, near_b, step_ref, msg_ref):
    layer, width = edge_a.shape
    layers = p_ref.shape[0] // layer
    half = width // 2
    high = place()[0] == 1
    odd = place()[1]
    total = c_ref[...]
    diag = d_ref[...]
    for k, (spot, edge, halo, there) in enumerate((
        ((1 - odd) * (layers - 1), edge_a, near_a, place()[2]),
        (odd * (layers - 1), edge_b, near_b, place()[3]),
    )):
        rows = pl.ds(pl.multiple_of(spot * layer, layer), layer)
        v = edge[...]
        step = jnp.where(there == 1, v - halo[...], 0.0)
        step_ref[k * layer:(k + 1) * layer, :] = step
        diag = diag + jnp.sum((step * v).reshape(layer // 8, 8, width), axis=0)
        peer = p_ref[rows, :]
        total = total + gram(jnp.where(high, peer, step), jnp.where(high, step, peer))
    msg_ref[:half, :] = jnp.where(high, total[half:], total[:half])
    msg_ref[half:, :] = jnp.broadcast_to(jnp.sum(diag, axis=0, keepdims=True), (8, width))


def beside(value):
    return jnp.concatenate(halves(value), axis=1)


def down_product(high, low, right):
    width = right.shape[1]
    both = beside(right)
    total = jnp.dot(high, both, preferred_element_type=F32)
    return total[:, :width] + (
        total[:, width:] + jnp.dot(low, both[:, :width], preferred_element_type=F32)
    )


def near_kernel(layer, cells_z, wo, own_step, peer_step, *refs):
    chunks = refs[:CHUNKS]
    xp, out, high_t, low_t, wp = refs[CHUNKS:]
    width = xp.shape[1]
    layers = xp.shape[0] // layer
    odd = place()[1]

    def at(j):
        return xp[j * layer:(j + 1) * layer, :]

    for i in range(layers):
        wp[i * layer:(i + 1) * layer, :] = inner_image(at, i, layers, cells_z)
    for k, spot in enumerate(((1 - odd) * (layers - 1), odd * (layers - 1))):
        rows = pl.ds(pl.multiple_of(spot * layer, layer), layer)
        wp[rows, :] += peer_step[k * layer:(k + 1) * layer, :]
    for i in range(layers):
        rows = slice(i * layer, (i + 1) * layer)
        image = wo[rows, :]
        for k in range(2):
            if i in (0, layers - 1):
                here = ((1 - odd), odd)[k] * (layers - 1) == i
                image = image + jnp.where(here, own_step[k * layer:(k + 1) * layer, :], 0.0)
        left = jnp.concatenate([image.T, wp[rows, :].T], axis=0)
        high_t[:, rows], low_t[:, rows] = halves(left)
    own = jnp.concatenate([chunk[...] for chunk in chunks], axis=0)
    for k, value in enumerate((own, xp[...])):
        out[:, k * width:(k + 1) * width] = down_product(high_t[...], low_t[...], value)


def far_kernel(high_t, low_t, far_own, out):
    out[...] = down_product(high_t[...], low_t[...], far_own[...])


def edges_kernel(x_ref, edge_a, edge_b, sems):
    layer = edge_a.shape[0]
    last = x_ref.shape[0] - layer
    odd = place()[1]
    copies = [
        pltpu.make_async_copy(x_ref.at[pl.ds(pl.multiple_of(start, layer), layer)], out, sems.at[k])
        for k, (start, out) in enumerate((((1 - odd) * last, edge_a), (odd * last, edge_b)))
    ]
    for copy in copies:
        copy.start()
    for copy in copies:
        copy.wait()


def eye_of(width):
    row = lax.broadcasted_iota(jnp.int32, (width, width), 0)
    col = lax.broadcasted_iota(jnp.int32, (width, width), 1)
    return jnp.where(row == col, 1.0, 0.0).astype(F32)


def rotations(pairs, high, x_ref):
    width = pairs[0][0].shape[1]
    half = width // 2
    eye = eye_of(width)
    ratios, normals = [], []
    for own, other in pairs:
        cross = jnp.concatenate(
            [jnp.where(high, other[:half], own[:half]), jnp.where(high, own[:half], other[:half])], axis=0
        )
        cross = jnp.where(high, cross.T, cross)
        rows = jnp.broadcast_to(own[half:half + 1], (width, width)).T
        ratio = cross / (rows + other[half:half + 1])
        ratios.append(ratio)
        normals.append(eye + product(ratio, ratio.T))
    bound = jnp.max(jnp.sum(jnp.abs(normals[0]), axis=0, keepdims=True), axis=1, keepdims=True)
    for normal in normals[1:]:
        size = jnp.max(jnp.sum(jnp.abs(normal), axis=0, keepdims=True), axis=1, keepdims=True)
        bound = jnp.maximum(bound, size)
    scale = 2.0 / (bound + 1.0)
    err = (bound - 1.0) * (0.5 * scale)

    def next_of(err):
        fresh = 2.0 / (2.0 - err * err)
        return err * err * (0.5 * fresh), fresh

    err, fresh = next_of(err)
    boths = []
    for normal in normals:
        image = scale * normal
        turn = fresh * (2.0 * eye - image)
        boths.append(jnp.concatenate([scale * turn, product_3(turn, image)], axis=1))
    for _ in range(STEPS - 1):
        err, fresh = next_of(err)
        boths = [product_3(fresh * (2.0 * eye - both[:, width:]), both) for both in boths]
    for k, both in enumerate(boths):
        x_ref[k] = both

    def step(err):
        err, fresh = next_of(err)
        for k in range(len(pairs)):
            both = x_ref[k]
            x_ref[k] = product_3(fresh * (2.0 * eye - both[:, width:]), both)
        return err

    lax.while_loop(lambda err: err > CLOSE, step, jnp.max(err))

    def refine(_=None):
        size = 0.0
        for k, (ratio, normal) in enumerate(zip(ratios, normals)):
            inverse = x_ref[k, :, :width]
            left_over = eye - product(inverse, normal)
            both = jnp.concatenate([inverse, product(inverse, ratio)], axis=1)
            x_ref[k] = both + product_3(left_over, both)
            size = jnp.maximum(size, jnp.max(jnp.sum(jnp.abs(left_over), axis=0)))
        return size

    lax.while_loop(lambda size: size > CLOSE, refine, refine())
    sign = jnp.where(high, 2.0, -2.0)
    return [
        (2.0 * x_ref[k, :, :width] - eye, sign * x_ref[k, :, width:]) for k in range(len(pairs))
    ]


def first_kernel(own_msg, core_msg, y_msg, far_msg, own_t, far_t, x_ref):
    width = own_msg.shape[1]
    pairs = [(own_msg[...], core_msg[...]), (y_msg[...], far_msg[...])]
    for (keep, take), out in zip(rotations(pairs, place()[0] == 1, x_ref), (own_t, far_t)):
        out[:, :width] = keep
        out[:, width:] = take


def apply_kernel(near_ref, far_ref, far_peer_ref, own_t, far_t, msg_ref):
    width = far_ref.shape[1]
    half = width // 2
    y_high = place()[4] == 1
    turn, far_turn = own_t[...], far_t[...]
    far_peer = jnp.concatenate([far_peer_ref[width:, :], far_peer_ref[:width, :]], axis=0)
    part = product_3(turn, jnp.concatenate([near_ref[...], far_ref[...], far_peer], axis=1))
    inside = turn * part[:, :2 * width]
    inside_high, inside_low = halves(inside)
    ones = jnp.ones((16, 2 * width), BF16)

    def lanes(value):
        return lax.dot_general(ones, value, (((1,), (1,)), ((), ())), preferred_element_type=F32)

    diag = lanes(inside_high) + lanes(inside_low)
    part = part[:, 2 * width:]
    cross = product_nt(jnp.where(y_high, far_turn, part), jnp.where(y_high, part, far_turn))
    msg_ref[:half, :] = jnp.where(y_high, cross[half:], cross[:half])
    msg_ref[half:, :] = diag[:8]


def wide_product(high_part, low_part, m_ref):
    width = m_ref.shape[1] // 2
    both = jnp.dot(high_part, m_ref[...], preferred_element_type=F32)
    rest = jnp.dot(low_part, m_ref[:, :width], preferred_element_type=F32)
    return both[:, :width] + (both[:, width:] + rest)


def turn_kernel(*refs):
    chunks = refs[:CHUNKS]
    xp, far_own, far_peer, own_t, far_t, high_ref, low_ref, m_ref = refs[CHUNKS:]
    width = xp.shape[1]
    step = 256
    for k, turn in enumerate((own_t, far_t)):
        m_ref[k, :, :width], m_ref[k, :, width:] = halves(
            jnp.concatenate([turn[:, :width].T, turn[:, width:].T], axis=0)
        )

    for i in range(xp.shape[0] // step):
        rows = slice(i * step, (i + 1) * step)
        ones = (rows_of(chunks, i * step, step), far_own[rows, :])
        for k, (one, two) in enumerate(zip(ones, (xp, far_peer))):
            parts = halves(jnp.concatenate([one, two[rows, :]], axis=1))
            turned = wide_product(*parts, m_ref.at[k])
            columns = slice(k * width, (k + 1) * width)
            high_ref[rows, columns], low_ref[rows, columns] = halves(turned)


def last_kernel(own_msg, y_msg, high_ref, low_ref, out, x_ref, m_ref, o_ref, sems):
    width = own_msg.shape[1]
    ((keep, take),) = rotations([(own_msg[...], y_msg[...])], place()[4] == 1, x_ref)
    m_ref[:, :width], m_ref[:, width:] = halves(jnp.concatenate([keep, take.T], axis=0))
    step = o_ref.shape[1]
    copies = []
    for k in range(o_ref.shape[0]):
        rows = slice(k * step, (k + 1) * step)
        o_ref[k] = wide_product(high_ref[rows, :], low_ref[rows, :], m_ref)
        copies.append(pltpu.make_async_copy(o_ref.at[k], out.at[pl.ds(k * step, step)], sems.at[k]))
        copies[-1].start()
    for copy in copies:
        copy.wait()


def power_of_two(count):
    return count & (count - 1) == 0


def summed_over_space(value, beside_it):
    count = lax.axis_size("space")
    blocks = lax.axis_size("blk")
    if not power_of_two(count):
        value = lax.psum(value, "space")
        beside_it([value])
        return value
    bits = [1 << bit for bit in range(count.bit_length() - 1)]
    orders = (bits, bits[-1:] + bits[:-1])
    sums = []
    for step in range(len(bits)):
        route = [
            (i * blocks + j, (i ^ orders[j & 1][step]) * blocks + j) for i in range(count) for j in range(blocks)
        ]
        there = lax.ppermute(value, ("space", "blk"), route)
        if step == len(bits) - 1:
            value = lax.optimization_barrier((value, beside_it(sums)))[0]
        value = value + there
        sums.append(value)
    return value


def shards(snapshots):
    layers, cells_y, cells_z, width = snapshots.shape
    layer = cells_y * cells_z
    cells = layers * layer
    own = snapshots.reshape(cells, width)
    size = lax.axis_size("space")
    route_a = [(i, i ^ 1) for i in range(size) if i ^ 1 < size]
    route_b = [(i, j) for i in range(1, size - 1, 2) for j in (i + 1,)]
    route_b = route_b + [(j, i) for i, j in route_b]
    half_rows = width // 2 + 8

    def call(body, inputs, outputs, scratch, micros, name, **more):
        return pl.pallas_call(
            body,
            in_specs=[VMEM] * len(inputs),
            out_specs=[VMEM] * len(outputs),
            out_shape=outputs,
            scratch_shapes=scratch,
            compiler_params=PARAMS,
            cost_estimate=cost(micros),
            name=name,
            **more,
        )(*inputs)

    chunks = [own]
    peer = exchanged(own, "blk", 1)
    edge_a, edge_b = pl.pallas_call(
        edges_kernel,
        in_specs=[pl.BlockSpec(memory_space=pl.ANY)],
        out_specs=[VMEM] * 2,
        out_shape=[shape_of(layer, width)] * 2,
        scratch_shapes=[pltpu.SemaphoreType.DMA((2,))],
        compiler_params=pltpu.CompilerParams(vmem_limit_bytes=53 * 2**20),
        cost_estimate=cost(0.1),
        name="edges",
    )(own)
    near_a = lax.ppermute(edge_a, "space", route_a)
    near_b = lax.ppermute(edge_b, "space", route_b)
    far_own = exchanged(own, "blk", 2)

    image, cross, diag = call(
        lambda *refs: inner_kernel(cells_y, cells_z, *refs), [*chunks, peer],
        [shape_of(cells, width), shape_of(width, width), shape_of(8, width)], [], 0.1, "inner_grams",
    )
    steps, msg = call(
        edge_kernel, [edge_a, edge_b, peer, cross, diag, near_a, near_b],
        [shape_of(2 * layer, width), shape_of(half_rows, width)], [], 0.1, "edge_grams",
    )
    turned_down = jax.ShapeDtypeStruct((2 * width, cells), BF16)
    near = []

    def near_products(sums):
        peer_steps = exchanged(lax.optimization_barrier((steps, sums[0]))[0], "blk", 1)
        near[:] = call(
            functools.partial(near_kernel, layer, cells_z), [image, steps, peer_steps, *chunks, peer],
            [shape_of(2 * width, 2 * width), turned_down, turned_down], [pltpu.VMEM((cells, width), F32)],
            2.5, "near_grams",
        )
        return near[0]

    msg = summed_over_space(msg, near_products)
    near_grams, high_t, low_t = near
    core_msg, y_msg, far_msg = (exchanged(msg, "blk", mask) for mask in (1, 2, 3))
    (far_grams,) = call(
        far_kernel, [high_t, low_t, far_own], [shape_of(2 * width, width)], [], 0.7, "far_grams"
    )
    far_peer_grams = exchanged(far_grams, "blk", 1)
    msg, far_grams = lax.optimization_barrier((msg, far_grams))
    own_t, far_t = call(
        first_kernel, [msg, core_msg, y_msg, far_msg], [shape_of(width, 2 * width)] * 2,
        [pltpu.VMEM((2, width, 2 * width), F32)], 4, "first_rotation",
    )
    (msg,) = call(
        apply_kernel, [near_grams, far_grams, far_peer_grams, own_t, far_t],
        [shape_of(half_rows, width)], [], 1.2, "rotated_grams",
    )
    bits = jax.ShapeDtypeStruct((cells, 2 * width), BF16)
    turned = []

    def turn_blocks(sums):
        ready = lax.optimization_barrier((far_own, sums[0]))[0]
        far_peer = exchanged(ready, "blk", 1)
        turned[:] = call(
            turn_kernel, [*chunks, peer, ready, far_peer, own_t, far_t], [bits, bits],
            [pltpu.VMEM((2, 2 * width, 2 * width), BF16)], 1.4, "turned_blocks",
        )
        return turned[0]

    own_msg = summed_over_space(msg, turn_blocks)
    highs, lows = turned
    y_msg = exchanged(own_msg, "blk", 2)

    step = 512
    mixed = pl.pallas_call(
        last_kernel,
        in_specs=[VMEM] * 4,
        out_specs=pl.BlockSpec(memory_space=pl.ANY),
        out_shape=shape_of(cells, width),
        scratch_shapes=[
            pltpu.VMEM((1, width, 2 * width), F32),
            pltpu.VMEM((2 * width, 2 * width), BF16),
            pltpu.VMEM((cells // step, step, width), F32),
            pltpu.SemaphoreType.DMA((cells // step,)),
        ],
        compiler_params=PARAMS,
        cost_estimate=cost(4),
        name="last_rotation",
    )(own_msg, y_msg, highs, lows)
    return mixed.reshape(snapshots.shape)


def solution(mesh):
    return jax.shard_map(
        shards,
        mesh=mesh,
        in_specs=(P("space", None, None, "blk"),),
        out_specs=P("space", None, None, "blk"),
        check_vma=False,
    )
```

```python
import functools

import jax
import jax.numpy as jnp
from jax import lax
from jax.experimental import pallas as pl
from jax.experimental.pallas import tpu as pltpu
from jax.sharding import PartitionSpec as P

F32 = jnp.float32
BF16 = jnp.bfloat16
VMEM = pl.BlockSpec(memory_space=pltpu.VMEM)
PARAMS = pltpu.CompilerParams(vmem_limit_bytes=40 * 2**20)
CLOSE = 5e-4
STEPS = 5
CHUNKS = 1


def place():
    space = lax.axis_index("space")
    size = lax.axis_size("space")
    blk = lax.axis_index("blk")
    odd = space % 2
    has_a = jnp.where(odd == 1, 1, jnp.where(space < size - 1, 1, 0))
    has_b = jnp.where(odd == 1, jnp.where(space < size - 1, 1, 0), jnp.where(space > 0, 1, 0))
    return blk % 2, odd, has_a, has_b, (blk // 2) % 2


def cost(micros):
    return pl.CostEstimate(flops=int(micros * 1e9), bytes_accessed=1, transcendentals=0)


def rows_of(chunks, start, count):
    for chunk in chunks:
        if start < chunk.shape[0]:
            return chunk[start:start + count, :]
        start -= chunk.shape[0]


def shape_of(rows, width):
    return jax.ShapeDtypeStruct((rows, width), F32)


def exchanged(value, axis, mask):
    count = lax.axis_size(axis)
    return lax.ppermute(value, axis, [(i, i ^ mask) for i in range(count)])


def halves(value):
    high = value.astype(BF16)
    return high, (value - high.astype(F32)).astype(BF16)


def gram(left, right):
    def one(a, b):
        return lax.dot_general(a, b, (((0,), (0,)), ((), ())), preferred_element_type=F32)

    left_high, left_low = halves(left)
    right_high, right_low = halves(right)
    return one(left_high, right_high) + (one(left_high, right_low) + one(left_low, right_high))


def thirds(value):
    high = value.astype(BF16)
    rest = value - high.astype(F32)
    middle = rest.astype(BF16)
    return high, middle, (rest - middle.astype(F32)).astype(BF16)


def product(left, right):
    a, b, c = thirds(left)
    x, y, z = thirds(right)

    def pair(one, two, three, four):
        return jnp.dot(
            jnp.concatenate([one, two], axis=1), jnp.concatenate([three, four], axis=0),
            preferred_element_type=F32,
        )

    return pair(a, a, x, y) + (pair(b, a, x, z) + pair(c, b, x, y))


def product_3(left, right):
    left_high, left_low = halves(left)
    right_high, right_low = halves(right)
    deep = jnp.dot(
        jnp.concatenate([left_high, left_low], axis=1),
        jnp.concatenate([right_high, right_high], axis=0),
        preferred_element_type=F32,
    )
    return deep + jnp.dot(left_high, right_low, preferred_element_type=F32)


def product_nt(left, right):
    def one(a, b):
        return lax.dot_general(a, b, (((1,), (1,)), ((), ())), preferred_element_type=F32)

    left_high, left_low = halves(left)
    right_high, right_low = halves(right)
    return one(left_high, right_high) + (one(left_high, right_low) + one(left_low, right_high))


def inner_image(at, i, layers, cells_z):
    v = at(i)
    layer, width = v.shape
    place = lax.broadcasted_iota(jnp.int32, (layer, width), 0) % cells_z
    near = at(min(i + 1, layers - 1)) + at(max(i - 1, 0))
    near = near + jnp.concatenate([v[cells_z:], v[-cells_z:]], axis=0)
    near = near + jnp.concatenate([v[:cells_z], v[:-cells_z]], axis=0)
    near = near + jnp.where(place == cells_z - 1, v, pltpu.roll(v, layer - 1, 0))
    near = near + jnp.where(place == 0, v, pltpu.roll(v, 1, 0))
    return 7.0 * v - near


def inner_kernel(cells_y, cells_z, *refs):
    layer = cells_y * cells_z
    chunks = refs[:CHUNKS]
    p_ref, w_ref, c_ref, d_ref = refs[CHUNKS:]
    layers = p_ref.shape[0] // layer
    width = p_ref.shape[1]
    high = place()[0] == 1
    cross = jnp.zeros((width, width), F32)
    diag = jnp.zeros((8, width), F32)

    def at(j):
        return rows_of(chunks, j * layer, layer)

    for i in range(layers):
        rows = slice(i * layer, (i + 1) * layer)
        v = at(i)
        image = inner_image(at, i, layers, cells_z)
        w_ref[rows, :] = image
        diag += jnp.sum((image * v).reshape(layer // 8, 8, width), axis=0)
        peer = p_ref[rows, :]
        cross += gram(jnp.where(high, peer, image), jnp.where(high, image, peer))
    c_ref[...] = cross
    d_ref[...] = diag


def edge_kernel(edge_a, edge_b, p_ref, c_ref, d_ref, near_a, near_b, step_ref, msg_ref):
    layer, width = edge_a.shape
    layers = p_ref.shape[0] // layer
    half = width // 2
    high = place()[0] == 1
    odd = place()[1]
    total = c_ref[...]
    diag = d_ref[...]
    for k, (spot, edge, halo, there) in enumerate((
        ((1 - odd) * (layers - 1), edge_a, near_a, place()[2]),
        (odd * (layers - 1), edge_b, near_b, place()[3]),
    )):
        rows = pl.ds(pl.multiple_of(spot * layer, layer), layer)
        v = edge[...]
        step = jnp.where(there == 1, v - halo[...], 0.0)
        step_ref[k * layer:(k + 1) * layer, :] = step
        diag = diag + jnp.sum((step * v).reshape(layer // 8, 8, width), axis=0)
        peer = p_ref[rows, :]
        total = total + gram(jnp.where(high, peer, step), jnp.where(high, step, peer))
    msg_ref[:half, :] = jnp.where(high, total[half:], total[:half])
    msg_ref[half:, :] = jnp.broadcast_to(jnp.sum(diag, axis=0, keepdims=True), (8, width))


def beside(value):
    return jnp.concatenate(halves(value), axis=1)


def down_product(high, low, right):
    width = right.shape[1]
    both = beside(right)
    total = jnp.dot(high, both, preferred_element_type=F32)
    return total[:, :width] + (
        total[:, width:] + jnp.dot(low, both[:, :width], preferred_element_type=F32)
    )


def near_kernel(layer, cells_z, wo, own_step, peer_step, *refs):
    chunks = refs[:CHUNKS]
    xp, out, high_t, low_t, wp = refs[CHUNKS:]
    width = xp.shape[1]
    layers = xp.shape[0] // layer
    odd = place()[1]

    def at(j):
        return xp[j * layer:(j + 1) * layer, :]

    for i in range(layers):
        wp[i * layer:(i + 1) * layer, :] = inner_image(at, i, layers, cells_z)
    for k, spot in enumerate(((1 - odd) * (layers - 1), odd * (layers - 1))):
        rows = pl.ds(pl.multiple_of(spot * layer, layer), layer)
        wp[rows, :] += peer_step[k * layer:(k + 1) * layer, :]
    for i in range(layers):
        rows = slice(i * layer, (i + 1) * layer)
        image = wo[rows, :]
        for k in range(2):
            if i in (0, layers - 1):
                here = ((1 - odd), odd)[k] * (layers - 1) == i
                image = image + jnp.where(here, own_step[k * layer:(k + 1) * layer, :], 0.0)
        left = jnp.concatenate([image.T, wp[rows, :].T], axis=0)
        high_t[:, rows], low_t[:, rows] = halves(left)
    own = jnp.concatenate([chunk[...] for chunk in chunks], axis=0)
    for k, value in enumerate((own, xp[...])):
        out[:, k * width:(k + 1) * width] = down_product(high_t[...], low_t[...], value)


def far_kernel(high_t, low_t, far_own, out):
    out[...] = down_product(high_t[...], low_t[...], far_own[...])


def edges_kernel(x_ref, edge_a, edge_b, sems):
    layer = edge_a.shape[0]
    last = x_ref.shape[0] - layer
    odd = place()[1]
    copies = [
        pltpu.make_async_copy(x_ref.at[pl.ds(pl.multiple_of(start, layer), layer)], out, sems.at[k])
        for k, (start, out) in enumerate((((1 - odd) * last, edge_a), (odd * last, edge_b)))
    ]
    for copy in copies:
        copy.start()
    for copy in copies:
        copy.wait()


def eye_of(width):
    row = lax.broadcasted_iota(jnp.int32, (width, width), 0)
    col = lax.broadcasted_iota(jnp.int32, (width, width), 1)
    return jnp.where(row == col, 1.0, 0.0).astype(F32)


def rotations(pairs, high, x_ref):
    width = pairs[0][0].shape[1]
    half = width // 2
    eye = eye_of(width)
    ratios, normals = [], []
    for own, other in pairs:
        cross = jnp.concatenate(
            [jnp.where(high, other[:half], own[:half]), jnp.where(high, own[:half], other[:half])], axis=0
        )
        cross = jnp.where(high, cross.T, cross)
        rows = jnp.broadcast_to(own[half:half + 1], (width, width)).T
        ratio = cross / (rows + other[half:half + 1])
        ratios.append(ratio)
        normals.append(eye + product(ratio, ratio.T))
    bound = jnp.max(jnp.sum(jnp.abs(normals[0]), axis=0, keepdims=True), axis=1, keepdims=True)
    for normal in normals[1:]:
        size = jnp.max(jnp.sum(jnp.abs(normal), axis=0, keepdims=True), axis=1, keepdims=True)
        bound = jnp.maximum(bound, size)
    scale = 2.0 / (bound + 1.0)
    err = (bound - 1.0) * (0.5 * scale)

    def next_of(err):
        fresh = 2.0 / (2.0 - err * err)
        return err * err * (0.5 * fresh), fresh

    err, fresh = next_of(err)
    boths = []
    for normal in normals:
        image = scale * normal
        turn = fresh * (2.0 * eye - image)
        boths.append(jnp.concatenate([scale * turn, product_3(turn, image)], axis=1))
    for _ in range(STEPS - 1):
        err, fresh = next_of(err)
        boths = [product_3(fresh * (2.0 * eye - both[:, width:]), both) for both in boths]
    for k, both in enumerate(boths):
        x_ref[k] = both

    def step(err):
        err, fresh = next_of(err)
        for k in range(len(pairs)):
            both = x_ref[k]
            x_ref[k] = product_3(fresh * (2.0 * eye - both[:, width:]), both)
        return err

    lax.while_loop(lambda err: err > CLOSE, step, jnp.max(err))

    def refine(_=None):
        size = 0.0
        for k, (ratio, normal) in enumerate(zip(ratios, normals)):
            inverse = x_ref[k, :, :width]
            left_over = eye - product(inverse, normal)
            both = jnp.concatenate([inverse, product(inverse, ratio)], axis=1)
            x_ref[k] = both + product_3(left_over, both)
            size = jnp.maximum(size, jnp.max(jnp.sum(jnp.abs(left_over), axis=0)))
        return size

    lax.while_loop(lambda size: size > CLOSE, refine, refine())
    sign = jnp.where(high, 2.0, -2.0)
    return [
        (2.0 * x_ref[k, :, :width] - eye, sign * x_ref[k, :, width:]) for k in range(len(pairs))
    ]


def first_kernel(own_msg, core_msg, y_msg, far_msg, own_t, far_t, x_ref):
    width = own_msg.shape[1]
    pairs = [(own_msg[...], core_msg[...]), (y_msg[...], far_msg[...])]
    for (keep, take), out in zip(rotations(pairs, place()[0] == 1, x_ref), (own_t, far_t)):
        out[:, :width] = keep
        out[:, width:] = take


def apply_kernel(near_ref, far_ref, far_peer_ref, own_t, far_t, msg_ref):
    width = far_ref.shape[1]
    half = width // 2
    y_high = place()[4] == 1
    turn, far_turn = own_t[...], far_t[...]
    far_peer = jnp.concatenate([far_peer_ref[width:, :], far_peer_ref[:width, :]], axis=0)
    part = product_3(turn, jnp.concatenate([near_ref[...], far_ref[...], far_peer], axis=1))
    inside = turn * part[:, :2 * width]
    inside_high, inside_low = halves(inside)
    ones = jnp.ones((16, 2 * width), BF16)

    def lanes(value):
        return lax.dot_general(ones, value, (((1,), (1,)), ((), ())), preferred_element_type=F32)

    diag = lanes(inside_high) + lanes(inside_low)
    part = part[:, 2 * width:]
    cross = product_nt(jnp.where(y_high, far_turn, part), jnp.where(y_high, part, far_turn))
    msg_ref[:half, :] = jnp.where(y_high, cross[half:], cross[:half])
    msg_ref[half:, :] = diag[:8]


def wide_product(high_part, low_part, m_ref):
    width = m_ref.shape[1] // 2
    both = jnp.dot(high_part, m_ref[...], preferred_element_type=F32)
    rest = jnp.dot(low_part, m_ref[:, :width], preferred_element_type=F32)
    return both[:, :width] + (both[:, width:] + rest)


def turn_kernel(*refs):
    chunks = refs[:CHUNKS]
    xp, far_own, far_peer, own_t, far_t, high_ref, low_ref, m_ref = refs[CHUNKS:]
    width = xp.shape[1]
    step = 256
    for k, turn in enumerate((own_t, far_t)):
        m_ref[k, :, :width], m_ref[k, :, width:] = halves(
            jnp.concatenate([turn[:, :width].T, turn[:, width:].T], axis=0)
        )

    for i in range(xp.shape[0] // step):
        rows = slice(i * step, (i + 1) * step)
        ones = (rows_of(chunks, i * step, step), far_own[rows, :])
        for k, (one, two) in enumerate(zip(ones, (xp, far_peer))):
            parts = halves(jnp.concatenate([one, two[rows, :]], axis=1))
            turned = wide_product(*parts, m_ref.at[k])
            columns = slice(k * width, (k + 1) * width)
            high_ref[rows, columns], low_ref[rows, columns] = halves(turned)


def last_kernel(own_msg, y_msg, high_ref, low_ref, out, x_ref, m_ref, o_ref, sems):
    width = own_msg.shape[1]
    ((keep, take),) = rotations([(own_msg[...], y_msg[...])], place()[4] == 1, x_ref)
    m_ref[:, :width], m_ref[:, width:] = halves(jnp.concatenate([keep, take.T], axis=0))
    step = o_ref.shape[1]
    copies = []
    for k in range(o_ref.shape[0]):
        rows = slice(k * step, (k + 1) * step)
        o_ref[k] = wide_product(high_ref[rows, :], low_ref[rows, :], m_ref)
        copies.append(pltpu.make_async_copy(o_ref.at[k], out.at[pl.ds(k * step, step)], sems.at[k]))
        copies[-1].start()
    for copy in copies:
        copy.wait()


def power_of_two(count):
    return count & (count - 1) == 0


def summed_over(value, bits):
    if len(bits) == 1:
        return value + exchanged(value, "space", bits[0])
    one, two = bits
    near, far, both = (exchanged(value, "space", mask) for mask in (one, two, one | two))
    return (value + near) + (far + both)


def bits_of(count):
    return [1 << bit for bit in range(count.bit_length() - 1)]


def summed_but_one(value):
    count = lax.axis_size("space")
    if not power_of_two(count):
        return lax.psum(value, "space"), 0
    bits = bits_of(count)
    if len(bits) % 2 == 0:
        value = summed_over(value, bits[:1])
    for k in range(1 - len(bits) % 2, len(bits) - 1, 2):
        value = summed_over(value, bits[k:k + 2])
    return value, bits[-1]


def summed_over_space(value, beside_it):
    value, bit = summed_but_one(value)
    if bit == 0:
        return value
    there = exchanged(value, "space", bit)
    return lax.optimization_barrier((value, beside_it))[0] + there


def summed_with_y(value, bit, beside_it):
    if bit == 0:
        return value, exchanged(value, "blk", 2)
    count, blocks = lax.axis_size("space"), lax.axis_size("blk")
    there = exchanged(value, "space", bit)
    other = exchanged(value, "blk", 2)
    route = [(i * blocks + j, (i ^ bit) * blocks + (j ^ 2)) for i in range(count) for j in range(blocks)]
    other_there = lax.ppermute(value, ("space", "blk"), route)
    value, other = lax.optimization_barrier((value, other, beside_it))[:2]
    return value + there, other + other_there


def shards(snapshots):
    layers, cells_y, cells_z, width = snapshots.shape
    layer = cells_y * cells_z
    cells = layers * layer
    own = snapshots.reshape(cells, width)
    size = lax.axis_size("space")
    route_a = [(i, i ^ 1) for i in range(size) if i ^ 1 < size]
    route_b = [(i, j) for i in range(1, size - 1, 2) for j in (i + 1,)]
    route_b = route_b + [(j, i) for i, j in route_b]
    half_rows = width // 2 + 8

    def call(body, inputs, outputs, scratch, micros, name, **more):
        return pl.pallas_call(
            body,
            in_specs=[VMEM] * len(inputs),
            out_specs=[VMEM] * len(outputs),
            out_shape=outputs,
            scratch_shapes=scratch,
            compiler_params=PARAMS,
            cost_estimate=cost(micros),
            name=name,
            **more,
        )(*inputs)

    chunks = [own]
    peer = exchanged(own, "blk", 1)
    edge_a, edge_b = pl.pallas_call(
        edges_kernel,
        in_specs=[pl.BlockSpec(memory_space=pl.ANY)],
        out_specs=[VMEM] * 2,
        out_shape=[shape_of(layer, width)] * 2,
        scratch_shapes=[pltpu.SemaphoreType.DMA((2,))],
        compiler_params=pltpu.CompilerParams(vmem_limit_bytes=53 * 2**20),
        cost_estimate=cost(0.1),
        name="edges",
    )(own)
    near_a = lax.ppermute(edge_a, "space", route_a)
    near_b = lax.ppermute(edge_b, "space", route_b)
    far_own = exchanged(own, "blk", 2)

    image, cross, diag = call(
        lambda *refs: inner_kernel(cells_y, cells_z, *refs), [*chunks, peer],
        [shape_of(cells, width), shape_of(width, width), shape_of(8, width)], [], 0.1, "inner_grams",
    )
    steps, msg = call(
        edge_kernel, [edge_a, edge_b, peer, cross, diag, near_a, near_b],
        [shape_of(2 * layer, width), shape_of(half_rows, width)], [], 0.1, "edge_grams",
    )
    peer_steps = exchanged(steps, "blk", 1)
    turned_down = jax.ShapeDtypeStruct((2 * width, cells), BF16)
    near_grams, high_t, low_t = call(
        functools.partial(near_kernel, layer, cells_z), [image, steps, peer_steps, *chunks, peer],
        [shape_of(2 * width, 2 * width), turned_down, turned_down], [pltpu.VMEM((cells, width), F32)],
        2.5, "near_grams",
    )
    msg = summed_over_space(msg, near_grams)
    core_msg, y_msg, far_msg = (exchanged(msg, "blk", mask) for mask in (1, 2, 3))
    (far_grams,) = call(
        far_kernel, [high_t, low_t, far_own], [shape_of(2 * width, width)], [], 0.7, "far_grams"
    )
    far_peer_grams = exchanged(far_grams, "blk", 1)
    msg, far_grams = lax.optimization_barrier((msg, far_grams))
    own_t, far_t = call(
        first_kernel, [msg, core_msg, y_msg, far_msg], [shape_of(width, 2 * width)] * 2,
        [pltpu.VMEM((2, width, 2 * width), F32)], 4, "first_rotation",
    )
    (msg,) = call(
        apply_kernel, [near_grams, far_grams, far_peer_grams, own_t, far_t],
        [shape_of(half_rows, width)], [], 1.2, "rotated_grams",
    )
    msg, last = summed_but_one(msg)
    far_own = lax.optimization_barrier((far_own, msg))[0]
    far_peer = exchanged(far_own, "blk", 1)
    bits = jax.ShapeDtypeStruct((cells, 2 * width), BF16)
    highs, lows = call(
        turn_kernel, [*chunks, peer, far_own, far_peer, own_t, far_t], [bits, bits],
        [pltpu.VMEM((2, 2 * width, 2 * width), BF16)], 1.4, "turned_blocks",
    )
    own_msg, y_msg = summed_with_y(msg, last, highs)

    step = 512
    mixed = pl.pallas_call(
        last_kernel,
        in_specs=[VMEM] * 4,
        out_specs=pl.BlockSpec(memory_space=pl.ANY),
        out_shape=shape_of(cells, width),
        scratch_shapes=[
            pltpu.VMEM((1, width, 2 * width), F32),
            pltpu.VMEM((2 * width, 2 * width), BF16),
            pltpu.VMEM((cells // step, step, width), F32),
            pltpu.SemaphoreType.DMA((cells // step,)),
        ],
        compiler_params=PARAMS,
        cost_estimate=cost(4),
        name="last_rotation",
    )(own_msg, y_msg, highs, lows)
    return mixed.reshape(snapshots.shape)


def solution(mesh):
    return jax.shard_map(
        shards,
        mesh=mesh,
        in_specs=(P("space", None, None, "blk"),),
        out_specs=P("space", None, None, "blk"),
        check_vma=False,
    )
```

```python
import functools

import jax
import jax.numpy as jnp
from jax import lax
from jax.experimental import pallas as pl
from jax.experimental.pallas import tpu as pltpu
from jax.sharding import PartitionSpec as P

F32 = jnp.float32
BF16 = jnp.bfloat16
VMEM = pl.BlockSpec(memory_space=pltpu.VMEM)
PARAMS = pltpu.CompilerParams(vmem_limit_bytes=40 * 2**20)
CLOSE = 2e-3
STEPS = 5
CHUNKS = 1


def place():
    space = lax.axis_index("space")
    size = lax.axis_size("space")
    blk = lax.axis_index("blk")
    odd = space % 2
    has_a = jnp.where(odd == 1, 1, jnp.where(space < size - 1, 1, 0))
    has_b = jnp.where(odd == 1, jnp.where(space < size - 1, 1, 0), jnp.where(space > 0, 1, 0))
    return blk % 2, odd, has_a, has_b, (blk // 2) % 2


def cost(micros):
    return pl.CostEstimate(flops=int(micros * 1e9), bytes_accessed=1, transcendentals=0)


def rows_of(chunks, start, count):
    for chunk in chunks:
        if start < chunk.shape[0]:
            return chunk[start:start + count, :]
        start -= chunk.shape[0]


def shape_of(rows, width):
    return jax.ShapeDtypeStruct((rows, width), F32)


def exchanged(value, axis, mask):
    count = lax.axis_size(axis)
    return lax.ppermute(value, axis, [(i, i ^ mask) for i in range(count)])


def halves(value):
    high = value.astype(BF16)
    return high, (value - high.astype(F32)).astype(BF16)


def gram(left, right):
    def one(a, b):
        return lax.dot_general(a, b, (((0,), (0,)), ((), ())), preferred_element_type=F32)

    left_high, left_low = halves(left)
    right_high, right_low = halves(right)
    return one(left_high, right_high) + (one(left_high, right_low) + one(left_low, right_high))


def thirds(value):
    high = value.astype(BF16)
    rest = value - high.astype(F32)
    middle = rest.astype(BF16)
    return high, middle, (rest - middle.astype(F32)).astype(BF16)


def product(left, right):
    a, b, c = thirds(left)
    x, y, z = thirds(right)

    def pair(one, two, three, four):
        return jnp.dot(
            jnp.concatenate([one, two], axis=1), jnp.concatenate([three, four], axis=0),
            preferred_element_type=F32,
        )

    return pair(a, a, x, y) + (pair(b, a, x, z) + pair(c, b, x, y))


def product_3(left, right):
    left_high, left_low = halves(left)
    right_high, right_low = halves(right)
    deep = jnp.dot(
        jnp.concatenate([left_high, left_low], axis=1),
        jnp.concatenate([right_high, right_high], axis=0),
        preferred_element_type=F32,
    )
    return deep + jnp.dot(left_high, right_low, preferred_element_type=F32)


def product_nt(left, right):
    def one(a, b):
        return lax.dot_general(a, b, (((1,), (1,)), ((), ())), preferred_element_type=F32)

    left_high, left_low = halves(left)
    right_high, right_low = halves(right)
    return one(left_high, right_high) + (one(left_high, right_low) + one(left_low, right_high))


def inner_image(at, i, layers, cells_z):
    v = at(i)
    layer, width = v.shape
    place = lax.broadcasted_iota(jnp.int32, (layer, width), 0) % cells_z
    near = at(min(i + 1, layers - 1)) + at(max(i - 1, 0))
    near = near + jnp.concatenate([v[cells_z:], v[-cells_z:]], axis=0)
    near = near + jnp.concatenate([v[:cells_z], v[:-cells_z]], axis=0)
    near = near + jnp.where(place == cells_z - 1, v, pltpu.roll(v, layer - 1, 0))
    near = near + jnp.where(place == 0, v, pltpu.roll(v, 1, 0))
    return 7.0 * v - near


def inner_kernel(cells_y, cells_z, *refs):
    layer = cells_y * cells_z
    chunks = refs[:CHUNKS]
    p_ref, w_ref, c_ref, d_ref = refs[CHUNKS:]
    layers = p_ref.shape[0] // layer
    width = p_ref.shape[1]
    high = place()[0] == 1
    cross = jnp.zeros((width, width), F32)
    diag = jnp.zeros((8, width), F32)

    def at(j):
        return rows_of(chunks, j * layer, layer)

    for i in range(layers):
        rows = slice(i * layer, (i + 1) * layer)
        v = at(i)
        image = inner_image(at, i, layers, cells_z)
        w_ref[rows, :] = image
        diag += jnp.sum((image * v).reshape(layer // 8, 8, width), axis=0)
        peer = p_ref[rows, :]
        cross += gram(jnp.where(high, peer, image), jnp.where(high, image, peer))
    c_ref[...] = cross
    d_ref[...] = diag


def edge_kernel(edge_a, edge_b, p_ref, c_ref, d_ref, near_b, near_a, step_ref, msg_ref):
    layer, width = edge_a.shape
    layers = p_ref.shape[0] // layer
    half = width // 2
    high = place()[0] == 1
    odd = place()[1]
    total = c_ref[...]
    diag = d_ref[...]
    for k, (spot, edge, halo, there) in enumerate((
        ((1 - odd) * (layers - 1), edge_a, near_a, place()[2]),
        (odd * (layers - 1), edge_b, near_b, place()[3]),
    )):
        rows = pl.ds(pl.multiple_of(spot * layer, layer), layer)
        v = edge[...]
        step = jnp.where(there == 1, v - halo[...], 0.0)
        step_ref[k * layer:(k + 1) * layer, :] = step
        diag = diag + jnp.sum((step * v).reshape(layer // 8, 8, width), axis=0)
        peer = p_ref[rows, :]
        total = total + gram(jnp.where(high, peer, step), jnp.where(high, step, peer))
    msg_ref[:half, :] = jnp.where(high, total[half:], total[:half])
    msg_ref[half:, :] = jnp.broadcast_to(jnp.sum(diag, axis=0, keepdims=True), (8, width))


def beside(value):
    return jnp.concatenate(halves(value), axis=1)


def down_product(high, low, right):
    width = right.shape[1]
    both = beside(right)
    total = jnp.dot(high, both, preferred_element_type=F32)
    return total[:, :width] + (
        total[:, width:] + jnp.dot(low, both[:, :width], preferred_element_type=F32)
    )


def near_kernel(layer, cells_z, wo, own_step, peer_step, *refs):
    chunks = refs[:CHUNKS]
    xp, out, high_t, low_t, wp = refs[CHUNKS:]
    width = xp.shape[1]
    layers = xp.shape[0] // layer
    odd = place()[1]

    def at(j):
        return xp[j * layer:(j + 1) * layer, :]

    for i in range(layers):
        wp[i * layer:(i + 1) * layer, :] = inner_image(at, i, layers, cells_z)
    for k, spot in enumerate(((1 - odd) * (layers - 1), odd * (layers - 1))):
        rows = pl.ds(pl.multiple_of(spot * layer, layer), layer)
        wp[rows, :] += peer_step[k * layer:(k + 1) * layer, :]
    for i in range(layers):
        rows = slice(i * layer, (i + 1) * layer)
        image = wo[rows, :]
        for k in range(2):
            if i in (0, layers - 1):
                here = ((1 - odd), odd)[k] * (layers - 1) == i
                image = image + jnp.where(here, own_step[k * layer:(k + 1) * layer, :], 0.0)
        left = jnp.concatenate([image.T, wp[rows, :].T], axis=0)
        high_t[:, rows], low_t[:, rows] = halves(left)
    own = jnp.concatenate([chunk[...] for chunk in chunks], axis=0)
    for k, value in enumerate((own, xp[...])):
        out[:, k * width:(k + 1) * width] = down_product(high_t[...], low_t[...], value)


def far_kernel(high_t, low_t, far_own, out):
    out[...] = down_product(high_t[...], low_t[...], far_own[...])


def edges_kernel(x_ref, edge_a, edge_b, sems):
    layer = edge_a.shape[0]
    last = x_ref.shape[0] - layer
    odd = place()[1]
    copies = [
        pltpu.make_async_copy(x_ref.at[pl.ds(pl.multiple_of(start, layer), layer)], out, sems.at[k])
        for k, (start, out) in enumerate((((1 - odd) * last, edge_a), (odd * last, edge_b)))
    ]
    for copy in copies:
        copy.start()
    for copy in copies:
        copy.wait()


def eye_of(width):
    row = lax.broadcasted_iota(jnp.int32, (width, width), 0)
    col = lax.broadcasted_iota(jnp.int32, (width, width), 1)
    return jnp.where(row == col, 1.0, 0.0).astype(F32)


def rotations(pairs, high, x_ref, finish):
    width = pairs[0][0].shape[1]
    half = width // 2
    eye = eye_of(width)
    sign = jnp.where(high, 2.0, -2.0)
    ratios, normals = [], []
    for own, other in pairs:
        cross = jnp.concatenate(
            [jnp.where(high, other[:half], own[:half]), jnp.where(high, own[:half], other[:half])], axis=0
        )
        cross_t = cross.T
        own_diag, other_diag = own[half:half + 1], other[half:half + 1]
        own_rows = jnp.broadcast_to(own_diag, (width, width)).T
        other_rows = jnp.broadcast_to(other_diag, (width, width)).T
        ratio = jnp.where(high, cross_t, cross) / (own_rows + other_diag)
        ratio_t = jnp.where(high, cross, cross_t) / (other_rows + own_diag)
        ratios.append(ratio)
        normals.append(eye + product(ratio, ratio_t))
    bound = jnp.max(jnp.sum(jnp.abs(normals[0]), axis=0, keepdims=True), axis=1, keepdims=True)
    for normal in normals[1:]:
        size = jnp.max(jnp.sum(jnp.abs(normal), axis=0, keepdims=True), axis=1, keepdims=True)
        bound = jnp.maximum(bound, size)
    scale = 2.0 / (bound + 1.0)
    err = (bound - 1.0) * (0.5 * scale)

    def next_of(err):
        fresh = 2.0 / (2.0 - err * err)
        return err * err * (0.5 * fresh), fresh

    err, fresh = next_of(err)
    boths = []
    for normal in normals:
        image = scale * normal
        turn = fresh * (2.0 * eye - image)
        boths.append(jnp.concatenate([scale * turn, product_3(turn, image)], axis=1))
    for _ in range(STEPS - 1):
        err, fresh = next_of(err)
        boths = [product_3(fresh * (2.0 * eye - both[:, width:]), both) for both in boths]

    def refined(inverses):
        size = 0.0
        turns = []
        for k, (inverse, ratio, normal) in enumerate(zip(inverses, ratios, normals)):
            left_over = eye - product(inverse, normal)
            both = jnp.concatenate([inverse, product(inverse, ratio)], axis=1)
            both = both + product_3(left_over, both)
            x_ref[k] = both[:, :width]
            turns.append((2.0 * both[:, :width] - eye, sign * both[:, width:]))
            size = jnp.maximum(size, jnp.max(jnp.sum(jnp.abs(left_over), axis=0)))
        finish(turns)
        return size

    size = refined([both[:, :width] for both in boths])
    lax.while_loop(
        lambda size: size > CLOSE, lambda _: refined([x_ref[k] for k in range(len(pairs))]), size
    )


def first_kernel(far_msg, y_msg, core_msg, own_msg, own_t, far_t, x_ref):
    width = own_msg.shape[1]

    def finish(turns):
        for (keep, take), out in zip(turns, (own_t, far_t)):
            out[:, :width] = keep
            out[:, width:] = take

    pairs = [(own_msg[...], core_msg[...]), (y_msg[...], far_msg[...])]
    rotations(pairs, place()[0] == 1, x_ref, finish)


def apply_kernel(near_ref, far_ref, far_peer_ref, own_t, far_t, msg_ref):
    width = far_ref.shape[1]
    half = width // 2
    y_high = place()[4] == 1
    turn, far_turn = own_t[...], far_t[...]
    far_peer = jnp.concatenate([far_peer_ref[width:, :], far_peer_ref[:width, :]], axis=0)
    part = product_3(turn, jnp.concatenate([near_ref[...], far_ref[...], far_peer], axis=1))
    inside = turn * part[:, :2 * width]
    inside_high, inside_low = halves(inside)
    ones = jnp.ones((16, 2 * width), BF16)

    def lanes(value):
        return lax.dot_general(ones, value, (((1,), (1,)), ((), ())), preferred_element_type=F32)

    diag = lanes(inside_high) + lanes(inside_low)
    part = part[:, 2 * width:]
    cross = product_nt(jnp.where(y_high, far_turn, part), jnp.where(y_high, part, far_turn))
    msg_ref[:half, :] = jnp.where(y_high, cross[half:], cross[:half])
    msg_ref[half:, :] = diag[:8]


def wide_product(high_part, low_part, m_ref):
    width = m_ref.shape[1] // 2
    both = jnp.dot(high_part, m_ref[...], preferred_element_type=F32)
    rest = jnp.dot(low_part, m_ref[:, :width], preferred_element_type=F32)
    return both[:, :width] + (both[:, width:] + rest)


def turn_kernel(*refs):
    chunks = refs[:CHUNKS]
    xp, far_own, far_peer, own_t, far_t, high_ref, low_ref, m_ref = refs[CHUNKS:]
    width = xp.shape[1]
    step = 256
    for k, turn in enumerate((own_t, far_t)):
        m_ref[k, :, :width], m_ref[k, :, width:] = halves(
            jnp.concatenate([turn[:, :width].T, turn[:, width:].T], axis=0)
        )

    for i in range(xp.shape[0] // step):
        rows = slice(i * step, (i + 1) * step)
        ones = (rows_of(chunks, i * step, step), far_own[rows, :])
        for k, (one, two) in enumerate(zip(ones, (xp, far_peer))):
            parts = halves(jnp.concatenate([one, two[rows, :]], axis=1))
            turned = wide_product(*parts, m_ref.at[k])
            columns = slice(k * width, (k + 1) * width)
            high_ref[rows, columns], low_ref[rows, columns] = halves(turned)


def last_kernel(own_msg, y_msg, high_ref, low_ref, out, x_ref, m_ref, o_ref, sems):
    width = own_msg.shape[1]
    step = o_ref.shape[1]

    def finish(turns):
        keep, take = turns[0]
        m_ref[:, :width], m_ref[:, width:] = halves(jnp.concatenate([keep, take.T], axis=0))
        copies = []
        for k in range(o_ref.shape[0]):
            rows = slice(k * step, (k + 1) * step)
            o_ref[k] = wide_product(high_ref[rows, :], low_ref[rows, :], m_ref)
            copies.append(pltpu.make_async_copy(o_ref.at[k], out.at[pl.ds(k * step, step)], sems.at[k]))
            copies[-1].start()
        for copy in copies:
            copy.wait()

    rotations([(own_msg[...], y_msg[...])], place()[4] == 1, x_ref, finish)


def power_of_two(count):
    return count & (count - 1) == 0


def stages_of(count):
    bits = [1 << bit for bit in range(count.bit_length() - 1)]
    pairs = [tuple(bits[k:k + 2]) for k in range(0, len(bits) - 1, 2)]
    if len(bits) % 2 == 0:
        pairs[-1:] = [pairs[-1][:1]]
    return pairs + [(bits[-1],)]


def summed_over(value, stages):
    for bits in stages:
        if len(bits) == 1:
            value = value + exchanged(value, "space", bits[0])
        else:
            one, two = bits
            both, far, near = (exchanged(value, "space", mask) for mask in (one | two, two, one))
            value = (both + far) + (near + value)
    return value


def summed_over_space(value, beside_it):
    count = lax.axis_size("space")
    if not power_of_two(count):
        return lax.psum(value, "space")
    stages = stages_of(count)
    value = summed_over(value, stages[:-1])
    there = exchanged(value, "space", stages[-1][0])
    return lax.optimization_barrier((value, beside_it))[0] + there


def summed_with_y(value, beside_it):
    count, blocks = lax.axis_size("space"), lax.axis_size("blk")
    if not power_of_two(count):
        value = lax.psum(value, "space")
        return value, exchanged(value, "blk", 2)
    stages = stages_of(count)
    value = summed_over(value, stages[:-1])
    bit = stages[-1][0]
    route = [(i * blocks + j, (i ^ bit) * blocks + (j ^ 2)) for i in range(count) for j in range(blocks)]
    other_there = lax.ppermute(value, ("space", "blk"), route)
    there = exchanged(value, "space", bit)
    other = exchanged(value, "blk", 2)
    other_there, there, other = lax.optimization_barrier((other_there, there, other, beside_it))[:3]
    return value + there, other_there + other


def shards(snapshots):
    layers, cells_y, cells_z, width = snapshots.shape
    layer = cells_y * cells_z
    cells = layers * layer
    own = snapshots.reshape(cells, width)
    size = lax.axis_size("space")
    route_a = [(i, i ^ 1) for i in range(size) if i ^ 1 < size]
    route_b = [(i, j) for i in range(1, size - 1, 2) for j in (i + 1,)]
    route_b = route_b + [(j, i) for i, j in route_b]
    half_rows = width // 2 + 8

    def call(body, inputs, outputs, scratch, micros, name, **more):
        return pl.pallas_call(
            body,
            in_specs=[VMEM] * len(inputs),
            out_specs=[VMEM] * len(outputs),
            out_shape=outputs,
            scratch_shapes=scratch,
            compiler_params=PARAMS,
            cost_estimate=cost(micros),
            name=name,
            **more,
        )(*inputs)

    chunks = [own]
    peer = exchanged(own, "blk", 1)
    edge_a, edge_b = pl.pallas_call(
        edges_kernel,
        in_specs=[pl.BlockSpec(memory_space=pl.ANY)],
        out_specs=[VMEM] * 2,
        out_shape=[shape_of(layer, width)] * 2,
        scratch_shapes=[pltpu.SemaphoreType.DMA((2,))],
        compiler_params=pltpu.CompilerParams(vmem_limit_bytes=53 * 2**20),
        cost_estimate=cost(0.1),
        name="edges",
    )(own)
    near_a = lax.ppermute(edge_a, "space", route_a)
    near_b = lax.ppermute(edge_b, "space", route_b)
    far_own = exchanged(own, "blk", 2)

    image, cross, diag = call(
        lambda *refs: inner_kernel(cells_y, cells_z, *refs), [*chunks, peer],
        [shape_of(cells, width), shape_of(width, width), shape_of(8, width)], [], 0.1, "inner_grams",
    )
    steps, msg = call(
        edge_kernel, [edge_a, edge_b, peer, cross, diag, near_b, near_a],
        [shape_of(2 * layer, width), shape_of(half_rows, width)], [], 0.1, "edge_grams",
    )
    peer_steps = exchanged(steps, "blk", 1)
    turned_down = jax.ShapeDtypeStruct((2 * width, cells), BF16)
    near_grams, high_t, low_t = call(
        functools.partial(near_kernel, layer, cells_z), [image, steps, peer_steps, *chunks, peer],
        [shape_of(2 * width, 2 * width), turned_down, turned_down], [pltpu.VMEM((cells, width), F32)],
        2.5, "near_grams",
    )
    msg = summed_over_space(msg, near_grams)
    far_msg, y_msg, core_msg = (exchanged(msg, "blk", mask) for mask in (3, 2, 1))
    (far_grams,) = call(
        far_kernel, [high_t, low_t, far_own], [shape_of(2 * width, width)], [], 0.7, "far_grams"
    )
    far_peer_grams = exchanged(far_grams, "blk", 1)
    msg, far_grams = lax.optimization_barrier((msg, far_grams))
    own_t, far_t = call(
        first_kernel, [far_msg, y_msg, core_msg, msg], [shape_of(width, 2 * width)] * 2,
        [pltpu.VMEM((2, width, width), F32)], 4, "first_rotation",
    )
    (msg,) = call(
        apply_kernel, [near_grams, far_grams, far_peer_grams, own_t, far_t],
        [shape_of(half_rows, width)], [], 1.2, "rotated_grams",
    )
    far_own = lax.optimization_barrier((far_own, msg))[0]
    far_peer = exchanged(far_own, "blk", 1)
    bits = jax.ShapeDtypeStruct((cells, 2 * width), BF16)
    highs, lows = call(
        turn_kernel, [*chunks, peer, far_own, far_peer, own_t, far_t], [bits, bits],
        [pltpu.VMEM((2, 2 * width, 2 * width), BF16)], 1.4, "turned_blocks",
    )
    own_msg, y_msg = summed_with_y(msg, highs)

    step = 512
    mixed = pl.pallas_call(
        last_kernel,
        in_specs=[VMEM] * 4,
        out_specs=pl.BlockSpec(memory_space=pl.ANY),
        out_shape=shape_of(cells, width),
        scratch_shapes=[
            pltpu.VMEM((1, width, width), F32),
            pltpu.VMEM((2 * width, 2 * width), BF16),
            pltpu.VMEM((cells // step, step, width), F32),
            pltpu.SemaphoreType.DMA((cells // step,)),
        ],
        compiler_params=PARAMS,
        cost_estimate=cost(4),
        name="last_rotation",
    )(own_msg, y_msg, highs, lows)
    return mixed.reshape(snapshots.shape)


def solution(mesh):
    return jax.shard_map(
        shards,
        mesh=mesh,
        in_specs=(P("space", None, None, "blk"),),
        out_specs=P("space", None, None, "blk"),
        check_vma=False,
    )
```

```python
import functools

import jax
import jax.numpy as jnp
from jax import lax
from jax.experimental import pallas as pl
from jax.experimental.pallas import tpu as pltpu
from jax.sharding import PartitionSpec as P

F32 = jnp.float32
BF16 = jnp.bfloat16
VMEM = pl.BlockSpec(memory_space=pltpu.VMEM)
PARAMS = pltpu.CompilerParams(vmem_limit_bytes=40 * 2**20)
CLOSE = 2e-3
STEPS = 5
CHUNKS = 1


def place():
    space = lax.axis_index("space")
    size = lax.axis_size("space")
    blk = lax.axis_index("blk")
    odd = space % 2
    has_a = jnp.where(odd == 1, 1, jnp.where(space < size - 1, 1, 0))
    has_b = jnp.where(odd == 1, jnp.where(space < size - 1, 1, 0), jnp.where(space > 0, 1, 0))
    return blk % 2, odd, has_a, has_b, (blk // 2) % 2


def cost(micros):
    return pl.CostEstimate(flops=int(micros * 1e9), bytes_accessed=1, transcendentals=0)


def rows_of(chunks, start, count):
    for chunk in chunks:
        if start < chunk.shape[0]:
            return chunk[start:start + count, :]
        start -= chunk.shape[0]


def shape_of(rows, width):
    return jax.ShapeDtypeStruct((rows, width), F32)


def exchanged(value, axis, mask):
    count = lax.axis_size(axis)
    return lax.ppermute(value, axis, [(i, i ^ mask) for i in range(count)])


def halves(value):
    high = value.astype(BF16)
    return high, (value - high.astype(F32)).astype(BF16)


def gram(left, right):
    def one(a, b):
        return lax.dot_general(a, b, (((0,), (0,)), ((), ())), preferred_element_type=F32)

    left_high, left_low = halves(left)
    right_high, right_low = halves(right)
    return one(left_high, right_high) + (one(left_high, right_low) + one(left_low, right_high))


def thirds(value):
    high = value.astype(BF16)
    rest = value - high.astype(F32)
    middle = rest.astype(BF16)
    return high, middle, (rest - middle.astype(F32)).astype(BF16)


def product(left, right):
    a, b, c = thirds(left)
    x, y, z = thirds(right)

    def pair(one, two, three, four):
        return jnp.dot(
            jnp.concatenate([one, two], axis=1), jnp.concatenate([three, four], axis=0),
            preferred_element_type=F32,
        )

    return pair(a, a, x, y) + (pair(b, a, x, z) + pair(c, b, x, y))


def product_3(left, right):
    left_high, left_low = halves(left)
    right_high, right_low = halves(right)
    deep = jnp.dot(
        jnp.concatenate([left_high, left_low], axis=1),
        jnp.concatenate([right_high, right_high], axis=0),
        preferred_element_type=F32,
    )
    return deep + jnp.dot(left_high, right_low, preferred_element_type=F32)


def product_nt(left, right):
    def one(a, b):
        return lax.dot_general(a, b, (((1,), (1,)), ((), ())), preferred_element_type=F32)

    left_high, left_low = halves(left)
    right_high, right_low = halves(right)
    return one(left_high, right_high) + (one(left_high, right_low) + one(left_low, right_high))


def inner_image(at, i, layers, cells_z):
    v = at(i)
    layer, width = v.shape
    place = lax.broadcasted_iota(jnp.int32, (layer, width), 0) % cells_z
    near = at(min(i + 1, layers - 1)) + at(max(i - 1, 0))
    near = near + jnp.concatenate([v[cells_z:], v[-cells_z:]], axis=0)
    near = near + jnp.concatenate([v[:cells_z], v[:-cells_z]], axis=0)
    near = near + jnp.where(place == cells_z - 1, v, pltpu.roll(v, layer - 1, 0))
    near = near + jnp.where(place == 0, v, pltpu.roll(v, 1, 0))
    return 7.0 * v - near


def inner_kernel(cells_y, cells_z, *refs):
    layer = cells_y * cells_z
    chunks = refs[:CHUNKS]
    p_ref, w_ref, c_ref, d_ref = refs[CHUNKS:]
    layers = p_ref.shape[0] // layer
    width = p_ref.shape[1]
    high = place()[0] == 1
    cross = jnp.zeros((width, width), F32)
    diag = jnp.zeros((8, width), F32)

    def at(j):
        return rows_of(chunks, j * layer, layer)

    for i in range(layers):
        rows = slice(i * layer, (i + 1) * layer)
        v = at(i)
        image = inner_image(at, i, layers, cells_z)
        w_ref[rows, :] = image
        diag += jnp.sum((image * v).reshape(layer // 8, 8, width), axis=0)
        peer = p_ref[rows, :]
        cross += gram(jnp.where(high, peer, image), jnp.where(high, image, peer))
    c_ref[...] = cross
    d_ref[...] = diag


def edge_kernel(edge_a, edge_b, p_ref, c_ref, d_ref, near_a, near_b, step_ref, msg_ref):
    layer, width = edge_a.shape
    layers = p_ref.shape[0] // layer
    half = width // 2
    high = place()[0] == 1
    odd = place()[1]
    total = c_ref[...]
    diag = d_ref[...]
    for k, (spot, edge, halo, there) in enumerate((
        ((1 - odd) * (layers - 1), edge_a, near_a, place()[2]),
        (odd * (layers - 1), edge_b, near_b, place()[3]),
    )):
        rows = pl.ds(pl.multiple_of(spot * layer, layer), layer)
        v = edge[...]
        step = jnp.where(there == 1, v - halo[...], 0.0)
        step_ref[k * layer:(k + 1) * layer, :] = step
        diag = diag + jnp.sum((step * v).reshape(layer // 8, 8, width), axis=0)
        peer = p_ref[rows, :]
        total = total + gram(jnp.where(high, peer, step), jnp.where(high, step, peer))
    msg_ref[:half, :] = jnp.where(high, total[half:], total[:half])
    msg_ref[half:, :] = jnp.broadcast_to(jnp.sum(diag, axis=0, keepdims=True), (8, width))


def beside(value):
    return jnp.concatenate(halves(value), axis=1)


def down_product(high, low, right):
    width = right.shape[1]
    both = beside(right)
    total = jnp.dot(high, both, preferred_element_type=F32)
    return total[:, :width] + (
        total[:, width:] + jnp.dot(low, both[:, :width], preferred_element_type=F32)
    )


def near_kernel(layer, cells_z, wo, own_step, peer_step, *refs):
    chunks = refs[:CHUNKS]
    xp, out, high_t, low_t, wp = refs[CHUNKS:]
    width = xp.shape[1]
    layers = xp.shape[0] // layer
    odd = place()[1]

    def at(j):
        return xp[j * layer:(j + 1) * layer, :]

    for i in range(layers):
        wp[i * layer:(i + 1) * layer, :] = inner_image(at, i, layers, cells_z)
    for k, spot in enumerate(((1 - odd) * (layers - 1), odd * (layers - 1))):
        rows = pl.ds(pl.multiple_of(spot * layer, layer), layer)
        wp[rows, :] += peer_step[k * layer:(k + 1) * layer, :]
    for i in range(layers):
        rows = slice(i * layer, (i + 1) * layer)
        image = wo[rows, :]
        for k in range(2):
            if i in (0, layers - 1):
                here = ((1 - odd), odd)[k] * (layers - 1) == i
                image = image + jnp.where(here, own_step[k * layer:(k + 1) * layer, :], 0.0)
        left = jnp.concatenate([image.T, wp[rows, :].T], axis=0)
        high_t[:, rows], low_t[:, rows] = halves(left)
    own = jnp.concatenate([chunk[...] for chunk in chunks], axis=0)
    for k, value in enumerate((own, xp[...])):
        out[:, k * width:(k + 1) * width] = down_product(high_t[...], low_t[...], value)


def far_kernel(high_t, low_t, far_own, out):
    out[...] = down_product(high_t[...], low_t[...], far_own[...])


def edges_kernel(x_ref, edge_a, edge_b, sems):
    layer = edge_a.shape[0]
    last = x_ref.shape[0] - layer
    odd = place()[1]
    copies = [
        pltpu.make_async_copy(x_ref.at[pl.ds(pl.multiple_of(start, layer), layer)], out, sems.at[k])
        for k, (start, out) in enumerate((((1 - odd) * last, edge_a), (odd * last, edge_b)))
    ]
    for copy in copies:
        copy.start()
    for copy in copies:
        copy.wait()


def eye_of(width):
    row = lax.broadcasted_iota(jnp.int32, (width, width), 0)
    col = lax.broadcasted_iota(jnp.int32, (width, width), 1)
    return jnp.where(row == col, 1.0, 0.0).astype(F32)


def rotations(pairs, high, x_ref, finish):
    width = pairs[0][0].shape[1]
    half = width // 2
    eye = eye_of(width)
    sign = jnp.where(high, 2.0, -2.0)
    ratios, normals = [], []
    for own, other in pairs:
        cross = jnp.concatenate(
            [jnp.where(high, other[:half], own[:half]), jnp.where(high, own[:half], other[:half])], axis=0
        )
        cross_t = cross.T
        own_diag, other_diag = own[half:half + 1], other[half:half + 1]
        own_rows = jnp.broadcast_to(own_diag, (width, width)).T
        other_rows = jnp.broadcast_to(other_diag, (width, width)).T
        ratio = jnp.where(high, cross_t, cross) / (own_rows + other_diag)
        ratio_t = jnp.where(high, cross, cross_t) / (other_rows + own_diag)
        ratios.append(ratio)
        normals.append(eye + product(ratio, ratio_t))
    bound = jnp.max(jnp.sum(jnp.abs(normals[0]), axis=0, keepdims=True), axis=1, keepdims=True)
    for normal in normals[1:]:
        size = jnp.max(jnp.sum(jnp.abs(normal), axis=0, keepdims=True), axis=1, keepdims=True)
        bound = jnp.maximum(bound, size)
    scale = 2.0 / (bound + 1.0)
    err = (bound - 1.0) * (0.5 * scale)

    def next_of(err):
        fresh = 2.0 / (2.0 - err * err)
        return err * err * (0.5 * fresh), fresh

    err, fresh = next_of(err)
    boths = []
    for normal in normals:
        image = scale * normal
        turn = fresh * (2.0 * eye - image)
        boths.append(jnp.concatenate([scale * turn, product_3(turn, image)], axis=1))
    for _ in range(STEPS - 1):
        err, fresh = next_of(err)
        boths = [product_3(fresh * (2.0 * eye - both[:, width:]), both) for both in boths]

    def refined(inverses):
        size = 0.0
        turns = []
        for k, (inverse, ratio, normal) in enumerate(zip(inverses, ratios, normals)):
            left_over = eye - product(inverse, normal)
            both = jnp.concatenate([inverse, product(inverse, ratio)], axis=1)
            both = both + product_3(left_over, both)
            x_ref[k] = both[:, :width]
            turns.append((2.0 * both[:, :width] - eye, sign * both[:, width:]))
            size = jnp.maximum(size, jnp.max(jnp.sum(jnp.abs(left_over), axis=0)))
        finish(turns)
        return size

    size = refined([both[:, :width] for both in boths])
    lax.while_loop(
        lambda size: size > CLOSE, lambda _: refined([x_ref[k] for k in range(len(pairs))]), size
    )


def first_kernel(far_msg, y_msg, core_msg, own_msg, own_t, far_t, x_ref):
    width = own_msg.shape[1]

    def finish(turns):
        for (keep, take), out in zip(turns, (own_t, far_t)):
            out[:, :width] = keep
            out[:, width:] = take

    pairs = [(own_msg[...], core_msg[...]), (y_msg[...], far_msg[...])]
    rotations(pairs, place()[0] == 1, x_ref, finish)


def apply_kernel(near_ref, far_ref, far_peer_ref, own_t, far_t, msg_ref):
    width = far_ref.shape[1]
    half = width // 2
    y_high = place()[4] == 1
    turn, far_turn = own_t[...], far_t[...]
    far_peer = jnp.concatenate([far_peer_ref[width:, :], far_peer_ref[:width, :]], axis=0)
    part = product_3(turn, jnp.concatenate([near_ref[...], far_ref[...], far_peer], axis=1))
    inside = turn * part[:, :2 * width]
    inside_high, inside_low = halves(inside)
    ones = jnp.ones((16, 2 * width), BF16)

    def lanes(value):
        return lax.dot_general(ones, value, (((1,), (1,)), ((), ())), preferred_element_type=F32)

    diag = lanes(inside_high) + lanes(inside_low)
    part = part[:, 2 * width:]
    cross = product_nt(jnp.where(y_high, far_turn, part), jnp.where(y_high, part, far_turn))
    msg_ref[:half, :] = jnp.where(y_high, cross[half:], cross[:half])
    msg_ref[half:, :] = diag[:8]


def wide_product(high_part, low_part, m_ref):
    width = m_ref.shape[1] // 2
    both = jnp.dot(high_part, m_ref[...], preferred_element_type=F32)
    rest = jnp.dot(low_part, m_ref[:, :width], preferred_element_type=F32)
    return both[:, :width] + (both[:, width:] + rest)


def turn_kernel(*refs):
    chunks = refs[:CHUNKS]
    xp, far_own, far_peer, own_t, far_t, high_ref, low_ref, m_ref = refs[CHUNKS:]
    width = xp.shape[1]
    step = 256
    for k, turn in enumerate((own_t, far_t)):
        m_ref[k, :, :width], m_ref[k, :, width:] = halves(
            jnp.concatenate([turn[:, :width].T, turn[:, width:].T], axis=0)
        )

    for i in range(xp.shape[0] // step):
        rows = slice(i * step, (i + 1) * step)
        ones = (rows_of(chunks, i * step, step), far_own[rows, :])
        for k, (one, two) in enumerate(zip(ones, (xp, far_peer))):
            parts = halves(jnp.concatenate([one, two[rows, :]], axis=1))
            turned = wide_product(*parts, m_ref.at[k])
            columns = slice(k * width, (k + 1) * width)
            high_ref[rows, columns], low_ref[rows, columns] = halves(turned)


def last_kernel(own_msg, y_msg, high_ref, low_ref, out, x_ref, m_ref, o_ref, sems):
    width = own_msg.shape[1]
    step = o_ref.shape[1]

    def finish(turns):
        keep, take = turns[0]
        m_ref[:, :width], m_ref[:, width:] = halves(jnp.concatenate([keep, take.T], axis=0))
        copies = []
        for k in range(o_ref.shape[0]):
            rows = slice(k * step, (k + 1) * step)
            o_ref[k] = wide_product(high_ref[rows, :], low_ref[rows, :], m_ref)
            copies.append(pltpu.make_async_copy(o_ref.at[k], out.at[pl.ds(k * step, step)], sems.at[k]))
            copies[-1].start()
        for copy in copies:
            copy.wait()

    rotations([(own_msg[...], y_msg[...])], place()[4] == 1, x_ref, finish)


def power_of_two(count):
    return count & (count - 1) == 0


def stages_of(count):
    bits = [1 << bit for bit in range(count.bit_length() - 1)]
    pairs = [tuple(bits[k:k + 2]) for k in range(0, len(bits) - 1, 2)]
    if len(bits) % 2 == 0:
        pairs[-1:] = [pairs[-1][:1]]
    return pairs + [(bits[-1],)]


def summed_over(value, stages):
    for bits in stages:
        if len(bits) == 1:
            value = value + exchanged(value, "space", bits[0])
        else:
            one, two = bits
            both, far, near = (exchanged(value, "space", mask) for mask in (one | two, two, one))
            value = (both + far) + (near + value)
    return value


def summed_over_space(value, beside_it):
    count = lax.axis_size("space")
    if not power_of_two(count):
        return lax.psum(value, "space")
    stages = stages_of(count)
    value = summed_over(value, stages[:-1])
    there = exchanged(value, "space", stages[-1][0])
    return lax.optimization_barrier((value, beside_it))[0] + there


def summed_with_y(value, beside_it):
    count, blocks = lax.axis_size("space"), lax.axis_size("blk")
    if not power_of_two(count):
        value = lax.psum(value, "space")
        return value, exchanged(value, "blk", 2)
    stages = stages_of(count)
    value = summed_over(value, stages[:-1])
    bit = stages[-1][0]
    route = [(i * blocks + j, (i ^ bit) * blocks + (j ^ 2)) for i in range(count) for j in range(blocks)]
    other_there = lax.ppermute(value, ("space", "blk"), route)
    there = exchanged(value, "space", bit)
    other = exchanged(value, "blk", 2)
    other_there, there, other = lax.optimization_barrier((other_there, there, other, beside_it))[:3]
    return value + there, other_there + other


def shards(snapshots):
    layers, cells_y, cells_z, width = snapshots.shape
    layer = cells_y * cells_z
    cells = layers * layer
    own = snapshots.reshape(cells, width)
    size = lax.axis_size("space")
    route_a = [(i, i ^ 1) for i in range(size) if i ^ 1 < size]
    route_b = [(i, j) for i in range(1, size - 1, 2) for j in (i + 1,)]
    route_b = route_b + [(j, i) for i, j in route_b]
    half_rows = width // 2 + 8

    def call(body, inputs, outputs, scratch, micros, name, **more):
        return pl.pallas_call(
            body,
            in_specs=[VMEM] * len(inputs),
            out_specs=[VMEM] * len(outputs),
            out_shape=outputs,
            scratch_shapes=scratch,
            compiler_params=PARAMS,
            cost_estimate=cost(micros),
            name=name,
            **more,
        )(*inputs)

    chunks = [own]
    peer = exchanged(own, "blk", 1)
    edge_a, edge_b = pl.pallas_call(
        edges_kernel,
        in_specs=[pl.BlockSpec(memory_space=pl.ANY)],
        out_specs=[VMEM] * 2,
        out_shape=[shape_of(layer, width)] * 2,
        scratch_shapes=[pltpu.SemaphoreType.DMA((2,))],
        compiler_params=pltpu.CompilerParams(vmem_limit_bytes=53 * 2**20),
        cost_estimate=cost(0.1),
        name="edges",
    )(own)
    near_a = lax.ppermute(edge_a, "space", route_a)
    near_b = lax.ppermute(edge_b, "space", route_b)
    far_own = exchanged(own, "blk", 2)

    image, cross, diag = call(
        lambda *refs: inner_kernel(cells_y, cells_z, *refs), [*chunks, peer],
        [shape_of(cells, width), shape_of(width, width), shape_of(8, width)], [], 0.1, "inner_grams",
    )
    steps, msg = call(
        edge_kernel, [edge_a, edge_b, peer, cross, diag, near_a, near_b],
        [shape_of(2 * layer, width), shape_of(half_rows, width)], [], 0.1, "edge_grams",
    )
    peer_steps = exchanged(steps, "blk", 1)
    turned_down = jax.ShapeDtypeStruct((2 * width, cells), BF16)
    near_grams, high_t, low_t = call(
        functools.partial(near_kernel, layer, cells_z), [image, steps, peer_steps, *chunks, peer],
        [shape_of(2 * width, 2 * width), turned_down, turned_down], [pltpu.VMEM((cells, width), F32)],
        2.5, "near_grams",
    )
    msg = summed_over_space(msg, near_grams)
    far_msg, y_msg, core_msg = (exchanged(msg, "blk", mask) for mask in (3, 2, 1))
    (far_grams,) = call(
        far_kernel, [high_t, low_t, far_own], [shape_of(2 * width, width)], [], 0.7, "far_grams"
    )
    far_peer_grams = exchanged(far_grams, "blk", 1)
    msg, far_grams = lax.optimization_barrier((msg, far_grams))
    own_t, far_t = call(
        first_kernel, [far_msg, y_msg, core_msg, msg], [shape_of(width, 2 * width)] * 2,
        [pltpu.VMEM((2, width, width), F32)], 4, "first_rotation",
    )
    (msg,) = call(
        apply_kernel, [near_grams, far_grams, far_peer_grams, own_t, far_t],
        [shape_of(half_rows, width)], [], 1.2, "rotated_grams",
    )
    far_own = lax.optimization_barrier((far_own, msg))[0]
    far_peer = exchanged(far_own, "blk", 1)
    bits = jax.ShapeDtypeStruct((cells, 2 * width), BF16)
    highs, lows = call(
        turn_kernel, [*chunks, peer, far_own, far_peer, own_t, far_t], [bits, bits],
        [pltpu.VMEM((2, 2 * width, 2 * width), BF16)], 1.4, "turned_blocks",
    )
    own_msg, y_msg = summed_with_y(msg, highs)

    step = 512
    mixed = pl.pallas_call(
        last_kernel,
        in_specs=[VMEM] * 4,
        out_specs=pl.BlockSpec(memory_space=pl.ANY),
        out_shape=shape_of(cells, width),
        scratch_shapes=[
            pltpu.VMEM((1, width, width), F32),
            pltpu.VMEM((2 * width, 2 * width), BF16),
            pltpu.VMEM((cells // step, step, width), F32),
            pltpu.SemaphoreType.DMA((cells // step,)),
        ],
        compiler_params=PARAMS,
        cost_estimate=cost(4),
        name="last_rotation",
    )(own_msg, y_msg, highs, lows)
    return mixed.reshape(snapshots.shape)


def solution(mesh):
    return jax.shard_map(
        shards,
        mesh=mesh,
        in_specs=(P("space", None, None, "blk"),),
        out_specs=P("space", None, None, "blk"),
        check_vma=False,
    )
```

```python
import functools

import jax
import jax.numpy as jnp
from jax import lax
from jax.experimental import pallas as pl
from jax.experimental.pallas import tpu as pltpu
from jax.sharding import PartitionSpec as P

F32 = jnp.float32
BF16 = jnp.bfloat16
VMEM = pl.BlockSpec(memory_space=pltpu.VMEM)
PARAMS = pltpu.CompilerParams(vmem_limit_bytes=40 * 2**20)
CLOSE = 2e-3
STEPS = 5
CHUNKS = 1


def place():
    space = lax.axis_index("space")
    size = lax.axis_size("space")
    blk = lax.axis_index("blk")
    odd = space % 2
    has_a = jnp.where(odd == 1, 1, jnp.where(space < size - 1, 1, 0))
    has_b = jnp.where(odd == 1, jnp.where(space < size - 1, 1, 0), jnp.where(space > 0, 1, 0))
    return blk % 2, odd, has_a, has_b, (blk // 2) % 2


def cost(micros):
    return pl.CostEstimate(flops=int(micros * 1e9), bytes_accessed=1, transcendentals=0)


def rows_of(chunks, start, count):
    for chunk in chunks:
        if start < chunk.shape[0]:
            return chunk[start:start + count, :]
        start -= chunk.shape[0]


def shape_of(rows, width):
    return jax.ShapeDtypeStruct((rows, width), F32)


def exchanged(value, axis, mask):
    count = lax.axis_size(axis)
    return lax.ppermute(value, axis, [(i, i ^ mask) for i in range(count)])


def halves(value):
    high = value.astype(BF16)
    return high, (value - high.astype(F32)).astype(BF16)


def gram(left, right):
    def one(a, b):
        return lax.dot_general(a, b, (((0,), (0,)), ((), ())), preferred_element_type=F32)

    left_high, left_low = halves(left)
    right_high, right_low = halves(right)
    return one(left_high, right_high) + (one(left_high, right_low) + one(left_low, right_high))


def thirds(value):
    high = value.astype(BF16)
    rest = value - high.astype(F32)
    middle = rest.astype(BF16)
    return high, middle, (rest - middle.astype(F32)).astype(BF16)


def product(left, right):
    a, b, c = thirds(left)
    x, y, z = thirds(right)
    return jnp.dot(
        jnp.concatenate([c, b, a, b, a, a], axis=1), jnp.concatenate([x, y, z, x, y, x], axis=0),
        preferred_element_type=F32,
    )


def product_3(left, right):
    left_high, left_low = halves(left)
    right_high, right_low = halves(right)
    return jnp.dot(
        jnp.concatenate([left_low, left_high, left_high], axis=1),
        jnp.concatenate([right_high, right_low, right_high], axis=0),
        preferred_element_type=F32,
    )


def product_nt(left, right):
    def one(a, b):
        return lax.dot_general(a, b, (((1,), (1,)), ((), ())), preferred_element_type=F32)

    left_high, left_low = halves(left)
    right_high, right_low = halves(right)
    return one(left_high, right_high) + (one(left_high, right_low) + one(left_low, right_high))


def inner_image(at, i, layers, cells_z):
    v = at(i)
    layer, width = v.shape
    place = lax.broadcasted_iota(jnp.int32, (layer, width), 0) % cells_z
    near = at(min(i + 1, layers - 1)) + at(max(i - 1, 0))
    near = near + jnp.concatenate([v[cells_z:], v[-cells_z:]], axis=0)
    near = near + jnp.concatenate([v[:cells_z], v[:-cells_z]], axis=0)
    near = near + jnp.where(place == cells_z - 1, v, pltpu.roll(v, layer - 1, 0))
    near = near + jnp.where(place == 0, v, pltpu.roll(v, 1, 0))
    return 7.0 * v - near


def inner_kernel(cells_y, cells_z, *refs):
    layer = cells_y * cells_z
    chunks = refs[:CHUNKS]
    p_ref, w_ref, c_ref, d_ref = refs[CHUNKS:]
    layers = p_ref.shape[0] // layer
    width = p_ref.shape[1]
    high = place()[0] == 1
    cross = jnp.zeros((width, width), F32)
    diag = jnp.zeros((8, width), F32)

    def at(j):
        return rows_of(chunks, j * layer, layer)

    for i in range(layers):
        rows = slice(i * layer, (i + 1) * layer)
        v = at(i)
        image = inner_image(at, i, layers, cells_z)
        w_ref[rows, :] = image
        diag += jnp.sum((image * v).reshape(layer // 8, 8, width), axis=0)
        peer = p_ref[rows, :]
        cross += gram(jnp.where(high, peer, image), jnp.where(high, image, peer))
    c_ref[...] = cross
    d_ref[...] = diag


def edge_kernel(edge_a, edge_b, p_ref, c_ref, d_ref, near_a, near_b, step_ref, msg_ref):
    layer, width = edge_a.shape
    layers = p_ref.shape[0] // layer
    half = width // 2
    high = place()[0] == 1
    odd = place()[1]
    total = c_ref[...]
    diag = d_ref[...]
    for k, (spot, edge, halo, there) in enumerate((
        ((1 - odd) * (layers - 1), edge_a, near_a, place()[2]),
        (odd * (layers - 1), edge_b, near_b, place()[3]),
    )):
        rows = pl.ds(pl.multiple_of(spot * layer, layer), layer)
        v = edge[...]
        step = jnp.where(there == 1, v - halo[...], 0.0)
        step_ref[k * layer:(k + 1) * layer, :] = step
        diag = diag + jnp.sum((step * v).reshape(layer // 8, 8, width), axis=0)
        peer = p_ref[rows, :]
        total = total + gram(jnp.where(high, peer, step), jnp.where(high, step, peer))
    msg_ref[:half, :] = jnp.where(high, total[half:], total[:half])
    msg_ref[half:, :] = jnp.broadcast_to(jnp.sum(diag, axis=0, keepdims=True), (8, width))


def beside(value):
    return jnp.concatenate(halves(value), axis=1)


def down_product(high, low, right):
    width = right.shape[1]
    both = beside(right)
    total = jnp.dot(high, both, preferred_element_type=F32)
    return total[:, :width] + (
        total[:, width:] + jnp.dot(low, both[:, :width], preferred_element_type=F32)
    )


def near_kernel(layer, cells_z, wo, own_step, peer_step, *refs):
    chunks = refs[:CHUNKS]
    xp, out, high_t, low_t, wp = refs[CHUNKS:]
    width = xp.shape[1]
    layers = xp.shape[0] // layer
    odd = place()[1]

    def at(j):
        return xp[j * layer:(j + 1) * layer, :]

    for i in range(layers):
        wp[i * layer:(i + 1) * layer, :] = inner_image(at, i, layers, cells_z)
    for k, spot in enumerate(((1 - odd) * (layers - 1), odd * (layers - 1))):
        rows = pl.ds(pl.multiple_of(spot * layer, layer), layer)
        wp[rows, :] += peer_step[k * layer:(k + 1) * layer, :]
    for i in range(layers):
        rows = slice(i * layer, (i + 1) * layer)
        image = wo[rows, :]
        for k in range(2):
            if i in (0, layers - 1):
                here = ((1 - odd), odd)[k] * (layers - 1) == i
                image = image + jnp.where(here, own_step[k * layer:(k + 1) * layer, :], 0.0)
        left = jnp.concatenate([image.T, wp[rows, :].T], axis=0)
        high_t[:, rows], low_t[:, rows] = halves(left)
    own = jnp.concatenate([chunk[...] for chunk in chunks], axis=0)
    for k, value in enumerate((own, xp[...])):
        out[:, k * width:(k + 1) * width] = down_product(high_t[...], low_t[...], value)


def far_kernel(high_t, low_t, far_own, out):
    out[...] = down_product(high_t[...], low_t[...], far_own[...])


def edges_kernel(x_ref, edge_a, edge_b, sems):
    layer = edge_a.shape[0]
    last = x_ref.shape[0] - layer
    odd = place()[1]
    copies = [
        pltpu.make_async_copy(x_ref.at[pl.ds(pl.multiple_of(start, layer), layer)], out, sems.at[k])
        for k, (start, out) in enumerate((((1 - odd) * last, edge_a), (odd * last, edge_b)))
    ]
    for copy in copies:
        copy.start()
    for copy in copies:
        copy.wait()


def eye_of(width):
    row = lax.broadcasted_iota(jnp.int32, (width, width), 0)
    col = lax.broadcasted_iota(jnp.int32, (width, width), 1)
    return jnp.where(row == col, 1.0, 0.0).astype(F32)


def rotations(pairs, high, x_ref, finish):
    width = pairs[0][0].shape[1]
    half = width // 2
    eye = eye_of(width)
    sign = jnp.where(high, 2.0, -2.0)
    ratios, normals = [], []
    for own, other in pairs:
        cross = jnp.concatenate(
            [jnp.where(high, other[:half], own[:half]), jnp.where(high, own[:half], other[:half])], axis=0
        )
        cross_t = cross.T
        own_diag, other_diag = own[half:half + 1], other[half:half + 1]
        own_rows = jnp.broadcast_to(own_diag, (width, width)).T
        other_rows = jnp.broadcast_to(other_diag, (width, width)).T
        ratio = jnp.where(high, cross_t, cross) / (own_rows + other_diag)
        ratio_t = jnp.where(high, cross, cross_t) / (other_rows + own_diag)
        ratios.append(ratio)
        normals.append(eye + product(ratio, ratio_t))
    bound = jnp.max(jnp.sum(jnp.abs(normals[0]), axis=0, keepdims=True), axis=1, keepdims=True)
    for normal in normals[1:]:
        size = jnp.max(jnp.sum(jnp.abs(normal), axis=0, keepdims=True), axis=1, keepdims=True)
        bound = jnp.maximum(bound, size)
    scale = 2.0 / (bound + 1.0)
    err = (bound - 1.0) * (0.5 * scale)

    def next_of(err):
        fresh = 2.0 / (2.0 - err * err)
        return err * err * (0.5 * fresh), fresh

    err, fresh = next_of(err)
    boths = []
    for normal in normals:
        image = scale * normal
        turn = fresh * (2.0 * eye - image)
        boths.append(jnp.concatenate([scale * turn, product_3(turn, image)], axis=1))
    for _ in range(STEPS - 1):
        err, fresh = next_of(err)
        boths = [product_3(fresh * (2.0 * eye - both[:, width:]), both) for both in boths]

    def refined(inverses):
        size = 0.0
        turns = []
        for k, (inverse, ratio, normal) in enumerate(zip(inverses, ratios, normals)):
            left_over = eye - product(inverse, normal)
            both = jnp.concatenate([inverse, product(inverse, ratio)], axis=1)
            both = both + product_3(left_over, both)
            x_ref[k] = both[:, :width]
            turns.append((2.0 * both[:, :width] - eye, sign * both[:, width:]))
            size = jnp.maximum(size, jnp.max(jnp.sum(jnp.abs(left_over), axis=0)))
        finish(turns)
        return size

    size = refined([both[:, :width] for both in boths])
    lax.while_loop(
        lambda size: size > CLOSE, lambda _: refined([x_ref[k] for k in range(len(pairs))]), size
    )


def first_kernel(far_msg, y_msg, core_msg, own_msg, own_t, far_t, x_ref):
    width = own_msg.shape[1]

    def finish(turns):
        for (keep, take), out in zip(turns, (own_t, far_t)):
            out[:, :width] = keep
            out[:, width:] = take

    pairs = [(own_msg[...], core_msg[...]), (y_msg[...], far_msg[...])]
    rotations(pairs, place()[0] == 1, x_ref, finish)


def apply_kernel(near_ref, far_ref, far_peer_ref, own_t, far_t, msg_ref):
    width = far_ref.shape[1]
    half = width // 2
    y_high = place()[4] == 1
    turn, far_turn = own_t[...], far_t[...]
    far_peer = jnp.concatenate([far_peer_ref[width:, :], far_peer_ref[:width, :]], axis=0)
    part = product_3(turn, jnp.concatenate([near_ref[...], far_ref[...], far_peer], axis=1))
    inside = turn * part[:, :2 * width]
    inside_high, inside_low = halves(inside)
    ones = jnp.ones((16, 2 * width), BF16)

    def lanes(value):
        return lax.dot_general(ones, value, (((1,), (1,)), ((), ())), preferred_element_type=F32)

    diag = lanes(inside_high) + lanes(inside_low)
    part = part[:, 2 * width:]
    cross = product_nt(jnp.where(y_high, far_turn, part), jnp.where(y_high, part, far_turn))
    msg_ref[:half, :] = jnp.where(y_high, cross[half:], cross[:half])
    msg_ref[half:, :] = diag[:8]


def wide_product(high_part, low_part, m_ref):
    width = m_ref.shape[1] // 2
    both = jnp.dot(high_part, m_ref[...], preferred_element_type=F32)
    rest = jnp.dot(low_part, m_ref[:, :width], preferred_element_type=F32)
    return both[:, :width] + (both[:, width:] + rest)


def turn_kernel(*refs):
    chunks = refs[:CHUNKS]
    xp, far_own, far_peer, own_t, far_t, high_ref, low_ref, m_ref = refs[CHUNKS:]
    width = xp.shape[1]
    step = 256
    for k, turn in enumerate((own_t, far_t)):
        m_ref[k, :, :width], m_ref[k, :, width:] = halves(
            jnp.concatenate([turn[:, :width].T, turn[:, width:].T], axis=0)
        )

    for i in range(xp.shape[0] // step):
        rows = slice(i * step, (i + 1) * step)
        ones = (rows_of(chunks, i * step, step), far_own[rows, :])
        for k, (one, two) in enumerate(zip(ones, (xp, far_peer))):
            parts = halves(jnp.concatenate([one, two[rows, :]], axis=1))
            turned = wide_product(*parts, m_ref.at[k])
            columns = slice(k * width, (k + 1) * width)
            high_ref[rows, columns], low_ref[rows, columns] = halves(turned)


def last_kernel(own_msg, y_msg, high_ref, low_ref, out, x_ref, m_ref, o_ref, sems):
    width = own_msg.shape[1]
    step = o_ref.shape[1]

    def finish(turns):
        keep, take = turns[0]
        m_ref[:, :width], m_ref[:, width:] = halves(jnp.concatenate([keep, take.T], axis=0))
        copies = []
        for k in range(o_ref.shape[0]):
            rows = slice(k * step, (k + 1) * step)
            o_ref[k] = wide_product(high_ref[rows, :], low_ref[rows, :], m_ref)
            copies.append(pltpu.make_async_copy(o_ref.at[k], out.at[pl.ds(k * step, step)], sems.at[k]))
            copies[-1].start()
        for copy in copies:
            copy.wait()

    rotations([(own_msg[...], y_msg[...])], place()[4] == 1, x_ref, finish)


def power_of_two(count):
    return count & (count - 1) == 0


def stages_of(count):
    bits = [1 << bit for bit in range(count.bit_length() - 1)]
    pairs = [tuple(bits[k:k + 2]) for k in range(0, len(bits) - 1, 2)]
    if len(bits) % 2 == 0:
        pairs[-1:] = [pairs[-1][:1]]
    return pairs + [(bits[-1],)]


def summed_over(value, stages):
    for bits in stages:
        if len(bits) == 1:
            value = value + exchanged(value, "space", bits[0])
        else:
            one, two = bits
            both, far, near = (exchanged(value, "space", mask) for mask in (one | two, two, one))
            value = (both + far) + (near + value)
    return value


def summed_over_space(value, beside_it):
    count = lax.axis_size("space")
    if not power_of_two(count):
        return lax.psum(value, "space")
    stages = stages_of(count)
    value = summed_over(value, stages[:-1])
    there = exchanged(value, "space", stages[-1][0])
    return lax.optimization_barrier((value, beside_it))[0] + there


def summed_with_y(value, beside_it):
    count, blocks = lax.axis_size("space"), lax.axis_size("blk")
    if not power_of_two(count):
        value = lax.psum(value, "space")
        return value, exchanged(value, "blk", 2)
    stages = stages_of(count)
    value = summed_over(value, stages[:-1])
    bit = stages[-1][0]
    route = [(i * blocks + j, (i ^ bit) * blocks + (j ^ 2)) for i in range(count) for j in range(blocks)]
    other_there = lax.ppermute(value, ("space", "blk"), route)
    there = exchanged(value, "space", bit)
    other = exchanged(value, "blk", 2)
    other_there, there, other = lax.optimization_barrier((other_there, there, other, beside_it))[:3]
    return value + there, other_there + other


def shards(snapshots):
    layers, cells_y, cells_z, width = snapshots.shape
    layer = cells_y * cells_z
    cells = layers * layer
    own = snapshots.reshape(cells, width)
    size = lax.axis_size("space")
    route_a = [(i, i ^ 1) for i in range(size) if i ^ 1 < size]
    route_b = [(i, j) for i in range(1, size - 1, 2) for j in (i + 1,)]
    route_b = route_b + [(j, i) for i, j in route_b]
    half_rows = width // 2 + 8

    def call(body, inputs, outputs, scratch, micros, name, **more):
        return pl.pallas_call(
            body,
            in_specs=[VMEM] * len(inputs),
            out_specs=[VMEM] * len(outputs),
            out_shape=outputs,
            scratch_shapes=scratch,
            compiler_params=PARAMS,
            cost_estimate=cost(micros),
            name=name,
            **more,
        )(*inputs)

    chunks = [own]
    peer = exchanged(own, "blk", 1)
    edge_a, edge_b = pl.pallas_call(
        edges_kernel,
        in_specs=[pl.BlockSpec(memory_space=pl.ANY)],
        out_specs=[VMEM] * 2,
        out_shape=[shape_of(layer, width)] * 2,
        scratch_shapes=[pltpu.SemaphoreType.DMA((2,))],
        compiler_params=pltpu.CompilerParams(vmem_limit_bytes=53 * 2**20),
        cost_estimate=cost(0.1),
        name="edges",
    )(own)
    near_a = lax.ppermute(edge_a, "space", route_a)
    near_b = lax.ppermute(edge_b, "space", route_b)
    far_own = exchanged(own, "blk", 2)

    image, cross, diag = call(
        lambda *refs: inner_kernel(cells_y, cells_z, *refs), [*chunks, peer],
        [shape_of(cells, width), shape_of(width, width), shape_of(8, width)], [], 0.1, "inner_grams",
    )
    steps, msg = call(
        edge_kernel, [edge_a, edge_b, peer, cross, diag, near_a, near_b],
        [shape_of(2 * layer, width), shape_of(half_rows, width)], [], 0.1, "edge_grams",
    )
    peer_steps = exchanged(steps, "blk", 1)
    turned_down = jax.ShapeDtypeStruct((2 * width, cells), BF16)
    near_grams, high_t, low_t = call(
        functools.partial(near_kernel, layer, cells_z), [image, steps, peer_steps, *chunks, peer],
        [shape_of(2 * width, 2 * width), turned_down, turned_down], [pltpu.VMEM((cells, width), F32)],
        2.5, "near_grams",
    )
    msg = summed_over_space(msg, near_grams)
    far_msg, y_msg, core_msg = (exchanged(msg, "blk", mask) for mask in (3, 2, 1))
    (far_grams,) = call(
        far_kernel, [high_t, low_t, far_own], [shape_of(2 * width, width)], [], 0.7, "far_grams"
    )
    far_peer_grams = exchanged(far_grams, "blk", 1)
    msg, far_grams = lax.optimization_barrier((msg, far_grams))
    own_t, far_t = call(
        first_kernel, [far_msg, y_msg, core_msg, msg], [shape_of(width, 2 * width)] * 2,
        [pltpu.VMEM((2, width, width), F32)], 4, "first_rotation",
    )
    (msg,) = call(
        apply_kernel, [near_grams, far_grams, far_peer_grams, own_t, far_t],
        [shape_of(half_rows, width)], [], 1.2, "rotated_grams",
    )
    far_own = lax.optimization_barrier((far_own, msg))[0]
    far_peer = exchanged(far_own, "blk", 1)
    bits = jax.ShapeDtypeStruct((cells, 2 * width), BF16)
    highs, lows = call(
        turn_kernel, [*chunks, peer, far_own, far_peer, own_t, far_t], [bits, bits],
        [pltpu.VMEM((2, 2 * width, 2 * width), BF16)], 1.4, "turned_blocks",
    )
    own_msg, y_msg = summed_with_y(msg, highs)

    step = 512
    mixed = pl.pallas_call(
        last_kernel,
        in_specs=[VMEM] * 4,
        out_specs=pl.BlockSpec(memory_space=pl.ANY),
        out_shape=shape_of(cells, width),
        scratch_shapes=[
            pltpu.VMEM((1, width, width), F32),
            pltpu.VMEM((2 * width, 2 * width), BF16),
            pltpu.VMEM((cells // step, step, width), F32),
            pltpu.SemaphoreType.DMA((cells // step,)),
        ],
        compiler_params=PARAMS,
        cost_estimate=cost(4),
        name="last_rotation",
    )(own_msg, y_msg, highs, lows)
    return mixed.reshape(snapshots.shape)


def solution(mesh):
    return jax.shard_map(
        shards,
        mesh=mesh,
        in_specs=(P("space", None, None, "blk"),),
        out_specs=P("space", None, None, "blk"),
        check_vma=False,
    )
```

```python
import functools

import jax
import jax.numpy as jnp
from jax import lax
from jax.experimental import pallas as pl
from jax.experimental.pallas import tpu as pltpu
from jax.sharding import PartitionSpec as P

F32 = jnp.float32
BF16 = jnp.bfloat16
VMEM = pl.BlockSpec(memory_space=pltpu.VMEM)
PARAMS = pltpu.CompilerParams(vmem_limit_bytes=40 * 2**20)
CLOSE = 2e-3
STEPS = 5
CHUNKS = 1


def place():
    space = lax.axis_index("space")
    size = lax.axis_size("space")
    blk = lax.axis_index("blk")
    odd = space % 2
    has_a = jnp.where(odd == 1, 1, jnp.where(space < size - 1, 1, 0))
    has_b = jnp.where(odd == 1, jnp.where(space < size - 1, 1, 0), jnp.where(space > 0, 1, 0))
    return blk % 2, odd, has_a, has_b, (blk // 2) % 2


def cost(micros):
    return pl.CostEstimate(flops=int(micros * 1e9), bytes_accessed=1, transcendentals=0)


def rows_of(chunks, start, count):
    for chunk in chunks:
        if start < chunk.shape[0]:
            return chunk[start:start + count, :]
        start -= chunk.shape[0]


def shape_of(rows, width):
    return jax.ShapeDtypeStruct((rows, width), F32)


def exchanged(value, axis, mask):
    count = lax.axis_size(axis)
    return lax.ppermute(value, axis, [(i, i ^ mask) for i in range(count)])


def halves(value):
    high = value.astype(BF16)
    return high, (value - high.astype(F32)).astype(BF16)


def gram(left, right):
    def one(a, b):
        return lax.dot_general(a, b, (((0,), (0,)), ((), ())), preferred_element_type=F32)

    left_high, left_low = halves(left)
    right_high, right_low = halves(right)
    return one(left_high, right_high) + (one(left_high, right_low) + one(left_low, right_high))


def thirds(value):
    high = value.astype(BF16)
    rest = value - high.astype(F32)
    middle = rest.astype(BF16)
    return high, middle, (rest - middle.astype(F32)).astype(BF16)


def product(left, right):
    a, b, c = thirds(left)
    x, y, z = thirds(right)

    def pair(one, two, three, four):
        return jnp.dot(
            jnp.concatenate([one, two], axis=1), jnp.concatenate([three, four], axis=0),
            preferred_element_type=F32,
        )

    return pair(a, a, x, y) + (pair(b, a, x, z) + pair(c, b, x, y))


def product_3(left, right):
    left_high, left_low = halves(left)
    right_high, right_low = halves(right)
    deep = jnp.dot(
        jnp.concatenate([left_high, left_low], axis=1),
        jnp.concatenate([right_high, right_high], axis=0),
        preferred_element_type=F32,
    )
    return deep + jnp.dot(left_high, right_low, preferred_element_type=F32)


def product_nt(left, right):
    def one(a, b):
        return lax.dot_general(a, b, (((1,), (1,)), ((), ())), preferred_element_type=F32)

    left_high, left_low = halves(left)
    right_high, right_low = halves(right)
    return one(left_high, right_high) + (one(left_high, right_low) + one(left_low, right_high))


def inner_image(at, i, layers, cells_z):
    v = at(i)
    layer, width = v.shape
    place = lax.broadcasted_iota(jnp.int32, (layer, width), 0) % cells_z
    near = at(min(i + 1, layers - 1)) + at(max(i - 1, 0))
    near = near + jnp.concatenate([v[cells_z:], v[-cells_z:]], axis=0)
    near = near + jnp.concatenate([v[:cells_z], v[:-cells_z]], axis=0)
    near = near + jnp.where(place == cells_z - 1, v, pltpu.roll(v, layer - 1, 0))
    near = near + jnp.where(place == 0, v, pltpu.roll(v, 1, 0))
    return 7.0 * v - near


def inner_kernel(cells_y, cells_z, *refs):
    layer = cells_y * cells_z
    chunks = refs[:CHUNKS]
    p_ref, w_ref, c_ref, d_ref = refs[CHUNKS:]
    layers = p_ref.shape[0] // layer
    width = p_ref.shape[1]
    high = place()[0] == 1
    cross = jnp.zeros((width, width), F32)
    diag = jnp.zeros((8, width), F32)

    def at(j):
        return rows_of(chunks, j * layer, layer)

    for i in range(layers):
        rows = slice(i * layer, (i + 1) * layer)
        v = at(i)
        image = inner_image(at, i, layers, cells_z)
        w_ref[rows, :] = image
        diag += jnp.sum((image * v).reshape(layer // 8, 8, width), axis=0)
        peer = p_ref[rows, :]
        cross += gram(jnp.where(high, peer, image), jnp.where(high, image, peer))
    c_ref[...] = cross
    d_ref[...] = diag


def edge_kernel(edge_a, edge_b, p_ref, c_ref, d_ref, near_a, near_b, step_ref, msg_ref):
    layer, width = edge_a.shape
    layers = p_ref.shape[0] // layer
    half = width // 2
    high = place()[0] == 1
    odd = place()[1]
    total = c_ref[...]
    diag = d_ref[...]
    for k, (spot, edge, halo, there) in enumerate((
        ((1 - odd) * (layers - 1), edge_a, near_a, place()[2]),
        (odd * (layers - 1), edge_b, near_b, place()[3]),
    )):
        rows = pl.ds(pl.multiple_of(spot * layer, layer), layer)
        v = edge[...]
        step = jnp.where(there == 1, v - halo[...], 0.0)
        step_ref[k * layer:(k + 1) * layer, :] = step
        diag = diag + jnp.sum((step * v).reshape(layer // 8, 8, width), axis=0)
        peer = p_ref[rows, :]
        total = total + gram(jnp.where(high, peer, step), jnp.where(high, step, peer))
    msg_ref[:half, :] = jnp.where(high, total[half:], total[:half])
    msg_ref[half:, :] = jnp.broadcast_to(jnp.sum(diag, axis=0, keepdims=True), (8, width))


def beside(value):
    return jnp.concatenate(halves(value), axis=1)


def down_product(high, low, right):
    width = right.shape[1]
    both = beside(right)
    total = jnp.dot(high, both, preferred_element_type=F32)
    return total[:, :width] + (
        total[:, width:] + jnp.dot(low, both[:, :width], preferred_element_type=F32)
    )


def near_kernel(layer, cells_z, wo, own_step, peer_step, *refs):
    chunks = refs[:CHUNKS]
    xp, out, high_t, low_t, wp = refs[CHUNKS:]
    width = xp.shape[1]
    layers = xp.shape[0] // layer
    odd = place()[1]

    def at(j):
        return xp[j * layer:(j + 1) * layer, :]

    for i in range(layers):
        wp[i * layer:(i + 1) * layer, :] = inner_image(at, i, layers, cells_z)
    for k, spot in enumerate(((1 - odd) * (layers - 1), odd * (layers - 1))):
        rows = pl.ds(pl.multiple_of(spot * layer, layer), layer)
        wp[rows, :] += peer_step[k * layer:(k + 1) * layer, :]
    for i in range(layers):
        rows = slice(i * layer, (i + 1) * layer)
        image = wo[rows, :]
        for k in range(2):
            if i in (0, layers - 1):
                here = ((1 - odd), odd)[k] * (layers - 1) == i
                image = image + jnp.where(here, own_step[k * layer:(k + 1) * layer, :], 0.0)
        left = jnp.concatenate([image.T, wp[rows, :].T], axis=0)
        high_t[:, rows], low_t[:, rows] = halves(left)
    own = jnp.concatenate([chunk[...] for chunk in chunks], axis=0)
    for k, value in enumerate((own, xp[...])):
        out[:, k * width:(k + 1) * width] = down_product(high_t[...], low_t[...], value)


def far_kernel(high_t, low_t, far_own, out):
    out[...] = down_product(high_t[...], low_t[...], far_own[...])


def edges_kernel(x_ref, edge_a, edge_b, sems):
    layer = edge_a.shape[0]
    last = x_ref.shape[0] - layer
    odd = place()[1]
    copies = [
        pltpu.make_async_copy(x_ref.at[pl.ds(pl.multiple_of(start, layer), layer)], out, sems.at[k])
        for k, (start, out) in enumerate((((1 - odd) * last, edge_a), (odd * last, edge_b)))
    ]
    for copy in copies:
        copy.start()
    for copy in copies:
        copy.wait()


def eye_of(width):
    row = lax.broadcasted_iota(jnp.int32, (width, width), 0)
    col = lax.broadcasted_iota(jnp.int32, (width, width), 1)
    return jnp.where(row == col, 1.0, 0.0).astype(F32)


def rotations(pairs, high, x_ref, finish):
    width = pairs[0][0].shape[1]
    half = width // 2
    eye = eye_of(width)
    sign = jnp.where(high, 2.0, -2.0)
    ratios, normals = [], []
    for own, other in pairs:
        cross = jnp.concatenate(
            [jnp.where(high, other[:half], own[:half]), jnp.where(high, own[:half], other[:half])], axis=0
        )
        cross_t = cross.T
        own_diag, other_diag = own[half:half + 1], other[half:half + 1]
        own_rows = jnp.broadcast_to(own_diag, (width, width)).T
        other_rows = jnp.broadcast_to(other_diag, (width, width)).T
        ratio = jnp.where(high, cross_t, cross) / (own_rows + other_diag)
        ratio_t = jnp.where(high, cross, cross_t) / (other_rows + own_diag)
        ratios.append(ratio)
        normals.append(eye + product(ratio, ratio_t))
    bound = jnp.max(jnp.sum(jnp.abs(normals[0]), axis=0, keepdims=True), axis=1, keepdims=True)
    for normal in normals[1:]:
        size = jnp.max(jnp.sum(jnp.abs(normal), axis=0, keepdims=True), axis=1, keepdims=True)
        bound = jnp.maximum(bound, size)
    scale = 2.0 / (bound + 1.0)
    err = (bound - 1.0) * (0.5 * scale)

    def next_of(err):
        fresh = 2.0 / (2.0 - err * err)
        return err * err * (0.5 * fresh), fresh

    err, fresh = next_of(err)
    boths = []
    for normal in normals:
        image = scale * normal
        turn = fresh * (2.0 * eye - image)
        boths.append(jnp.concatenate([scale * turn, product_3(turn, image)], axis=1))
    for _ in range(STEPS - 1):
        err, fresh = next_of(err)
        boths = [product_3(fresh * (2.0 * eye - both[:, width:]), both) for both in boths]

    def refined(inverses):
        size = 0.0
        turns = []
        for k, (inverse, ratio, normal) in enumerate(zip(inverses, ratios, normals)):
            left_over = eye - product(inverse, normal)
            both = jnp.concatenate([inverse, product(inverse, ratio)], axis=1)
            both = both + product_3(left_over, both)
            x_ref[k] = both[:, :width]
            turns.append((2.0 * both[:, :width] - eye, sign * both[:, width:]))
            size = jnp.maximum(size, jnp.max(jnp.sum(jnp.abs(left_over), axis=0)))
        finish(turns)
        return size

    size = refined([both[:, :width] for both in boths])
    lax.while_loop(
        lambda size: size > CLOSE, lambda _: refined([x_ref[k] for k in range(len(pairs))]), size
    )


def first_kernel(far_msg, y_msg, core_msg, own_msg, own_t, far_t, x_ref):
    width = own_msg.shape[1]

    def finish(turns):
        for (keep, take), out in zip(turns, (own_t, far_t)):
            out[:, :width] = keep
            out[:, width:] = take

    pairs = [(own_msg[...], core_msg[...]), (y_msg[...], far_msg[...])]
    rotations(pairs, place()[0] == 1, x_ref, finish)


def apply_kernel(near_ref, far_ref, far_peer_ref, own_t, far_t, msg_ref):
    width = far_ref.shape[1]
    half = width // 2
    y_high = place()[4] == 1
    turn, far_turn = own_t[...], far_t[...]
    far_peer = jnp.concatenate([far_peer_ref[width:, :], far_peer_ref[:width, :]], axis=0)
    part = product_3(turn, jnp.concatenate([near_ref[...], far_ref[...], far_peer], axis=1))
    inside = turn * part[:, :2 * width]
    inside_high, inside_low = halves(inside)
    ones = jnp.ones((16, 2 * width), BF16)

    def lanes(value):
        return lax.dot_general(ones, value, (((1,), (1,)), ((), ())), preferred_element_type=F32)

    diag = lanes(inside_high) + lanes(inside_low)
    part = part[:, 2 * width:]
    cross = product_nt(jnp.where(y_high, far_turn, part), jnp.where(y_high, part, far_turn))
    msg_ref[:half, :] = jnp.where(y_high, cross[half:], cross[:half])
    msg_ref[half:, :] = diag[:8]


def wide_product(high_part, low_part, m_ref):
    width = m_ref.shape[1] // 2
    both = jnp.dot(high_part, m_ref[...], preferred_element_type=F32)
    rest = jnp.dot(low_part, m_ref[:, :width], preferred_element_type=F32)
    return both[:, :width] + (both[:, width:] + rest)


def turn_kernel(*refs):
    chunks = refs[:CHUNKS]
    xp, far_own, far_peer, own_t, far_t, high_ref, low_ref, m_ref = refs[CHUNKS:]
    width = xp.shape[1]
    step = 256
    for k, turn in enumerate((own_t, far_t)):
        m_ref[k, :, :width], m_ref[k, :, width:] = halves(
            jnp.concatenate([turn[:, :width].T, turn[:, width:].T], axis=0)
        )

    for i in range(xp.shape[0] // step):
        rows = slice(i * step, (i + 1) * step)
        ones = (rows_of(chunks, i * step, step), far_own[rows, :])
        for k, (one, two) in enumerate(zip(ones, (xp, far_peer))):
            parts = halves(jnp.concatenate([one, two[rows, :]], axis=1))
            turned = wide_product(*parts, m_ref.at[k])
            columns = slice(k * width, (k + 1) * width)
            high_ref[rows, columns], low_ref[rows, columns] = halves(turned)


def last_kernel(own_msg, y_msg, high_ref, low_ref, out, x_ref, m_ref, o_ref, sems):
    width = own_msg.shape[1]
    step = o_ref.shape[1]

    def finish(turns):
        keep, take = turns[0]
        m_ref[:, :width], m_ref[:, width:] = halves(jnp.concatenate([keep, take.T], axis=0))
        copies = []
        for k in range(o_ref.shape[0]):
            rows = slice(k * step, (k + 1) * step)
            o_ref[k] = wide_product(high_ref[rows, :], low_ref[rows, :], m_ref)
            copies.append(pltpu.make_async_copy(o_ref.at[k], out.at[pl.ds(k * step, step)], sems.at[k]))
            copies[-1].start()
        for copy in copies:
            copy.wait()

    rotations([(own_msg[...], y_msg[...])], place()[4] == 1, x_ref, finish)


def power_of_two(count):
    return count & (count - 1) == 0


def stages_of(bits):
    pairs = [tuple(bits[k:k + 2]) for k in range(0, len(bits) - 1, 2)]
    if len(bits) % 2 == 0:
        pairs[-1:] = [pairs[-1][:1]]
    return pairs + [(bits[-1],)]


def bits_of(count):
    return [1 << bit for bit in range(count.bit_length() - 1)]


def summed_over(value, stages):
    for bits in stages:
        if len(bits) == 1:
            value = value + exchanged(value, "space", bits[0])
        else:
            one, two = bits
            both, far, near = (exchanged(value, "space", mask) for mask in (one | two, two, one))
            value = (both + far) + (near + value)
    return value


def summed_over_space(value, beside_it):
    count = lax.axis_size("space")
    if not power_of_two(count):
        return lax.psum(value, "space")
    stages = stages_of(bits_of(count))
    value = summed_over(value, stages[:-1])
    there = exchanged(value, "space", stages[-1][0])
    return lax.optimization_barrier((value, beside_it))[0] + there


def summed_with_y(value, beside_it):
    count, blocks = lax.axis_size("space"), lax.axis_size("blk")
    if not power_of_two(count):
        value = lax.psum(value, "space")
        return value, exchanged(value, "blk", 2)
    bits = bits_of(count)
    stages = stages_of(bits[:1] + bits[2:] + bits[1:2])
    value = summed_over(value, stages[:-1])
    bit = stages[-1][0]
    route = [(i * blocks + j, (i ^ bit) * blocks + (j ^ 2)) for i in range(count) for j in range(blocks)]
    other_there = lax.ppermute(value, ("space", "blk"), route)
    there = exchanged(value, "space", bit)
    other = exchanged(value, "blk", 2)
    other_there, there, other = lax.optimization_barrier((other_there, there, other, beside_it))[:3]
    return value + there, other_there + other


def shards(snapshots):
    layers, cells_y, cells_z, width = snapshots.shape
    layer = cells_y * cells_z
    cells = layers * layer
    own = snapshots.reshape(cells, width)
    size = lax.axis_size("space")
    route_a = [(i, i ^ 1) for i in range(size) if i ^ 1 < size]
    route_b = [(i, j) for i in range(1, size - 1, 2) for j in (i + 1,)]
    route_b = route_b + [(j, i) for i, j in route_b]
    half_rows = width // 2 + 8

    def call(body, inputs, outputs, scratch, micros, name, **more):
        return pl.pallas_call(
            body,
            in_specs=[VMEM] * len(inputs),
            out_specs=[VMEM] * len(outputs),
            out_shape=outputs,
            scratch_shapes=scratch,
            compiler_params=PARAMS,
            cost_estimate=cost(micros),
            name=name,
            **more,
        )(*inputs)

    chunks = [own]
    peer = exchanged(own, "blk", 1)
    edge_a, edge_b = pl.pallas_call(
        edges_kernel,
        in_specs=[pl.BlockSpec(memory_space=pl.ANY)],
        out_specs=[VMEM] * 2,
        out_shape=[shape_of(layer, width)] * 2,
        scratch_shapes=[pltpu.SemaphoreType.DMA((2,))],
        compiler_params=pltpu.CompilerParams(vmem_limit_bytes=53 * 2**20),
        cost_estimate=cost(0.1),
        name="edges",
    )(own)
    near_a = lax.ppermute(edge_a, "space", route_a)
    near_b = lax.ppermute(edge_b, "space", route_b)
    far_own = exchanged(own, "blk", 2)

    image, cross, diag = call(
        lambda *refs: inner_kernel(cells_y, cells_z, *refs), [*chunks, peer],
        [shape_of(cells, width), shape_of(width, width), shape_of(8, width)], [], 0.1, "inner_grams",
    )
    steps, msg = call(
        edge_kernel, [edge_a, edge_b, peer, cross, diag, near_a, near_b],
        [shape_of(2 * layer, width), shape_of(half_rows, width)], [], 0.1, "edge_grams",
    )
    peer_steps = exchanged(steps, "blk", 1)
    turned_down = jax.ShapeDtypeStruct((2 * width, cells), BF16)
    near_grams, high_t, low_t = call(
        functools.partial(near_kernel, layer, cells_z), [image, steps, peer_steps, *chunks, peer],
        [shape_of(2 * width, 2 * width), turned_down, turned_down], [pltpu.VMEM((cells, width), F32)],
        2.5, "near_grams",
    )
    msg = summed_over_space(msg, near_grams)
    far_msg, y_msg, core_msg = (exchanged(msg, "blk", mask) for mask in (3, 2, 1))
    (far_grams,) = call(
        far_kernel, [high_t, low_t, far_own], [shape_of(2 * width, width)], [], 0.7, "far_grams"
    )
    far_peer_grams = exchanged(far_grams, "blk", 1)
    msg, far_grams = lax.optimization_barrier((msg, far_grams))
    own_t, far_t = call(
        first_kernel, [far_msg, y_msg, core_msg, msg], [shape_of(width, 2 * width)] * 2,
        [pltpu.VMEM((2, width, width), F32)], 4, "first_rotation",
    )
    (msg,) = call(
        apply_kernel, [near_grams, far_grams, far_peer_grams, own_t, far_t],
        [shape_of(half_rows, width)], [], 1.2, "rotated_grams",
    )
    far_own = lax.optimization_barrier((far_own, msg))[0]
    far_peer = exchanged(far_own, "blk", 1)
    bits = jax.ShapeDtypeStruct((cells, 2 * width), BF16)
    highs, lows = call(
        turn_kernel, [*chunks, peer, far_own, far_peer, own_t, far_t], [bits, bits],
        [pltpu.VMEM((2, 2 * width, 2 * width), BF16)], 1.4, "turned_blocks",
    )
    own_msg, y_msg = summed_with_y(msg, highs)

    step = 512
    mixed = pl.pallas_call(
        last_kernel,
        in_specs=[VMEM] * 4,
        out_specs=pl.BlockSpec(memory_space=pl.ANY),
        out_shape=shape_of(cells, width),
        scratch_shapes=[
            pltpu.VMEM((1, width, width), F32),
            pltpu.VMEM((2 * width, 2 * width), BF16),
            pltpu.VMEM((cells // step, step, width), F32),
            pltpu.SemaphoreType.DMA((cells // step,)),
        ],
        compiler_params=PARAMS,
        cost_estimate=cost(4),
        name="last_rotation",
    )(own_msg, y_msg, highs, lows)
    return mixed.reshape(snapshots.shape)


def solution(mesh):
    return jax.shard_map(
        shards,
        mesh=mesh,
        in_specs=(P("space", None, None, "blk"),),
        out_specs=P("space", None, None, "blk"),
        check_vma=False,
    )
```

```python
import functools

import jax
import jax.numpy as jnp
from jax import lax
from jax.experimental import pallas as pl
from jax.experimental.pallas import tpu as pltpu
from jax.sharding import PartitionSpec as P

F32 = jnp.float32
BF16 = jnp.bfloat16
VMEM = pl.BlockSpec(memory_space=pltpu.VMEM)
PARAMS = pltpu.CompilerParams(vmem_limit_bytes=40 * 2**20)
CLOSE = 2e-3
STEPS = 5
MORE = 8
CHUNKS = 1


def place():
    space = lax.axis_index("space")
    size = lax.axis_size("space")
    blk = lax.axis_index("blk")
    odd = space % 2
    has_a = jnp.where(odd == 1, 1, jnp.where(space < size - 1, 1, 0))
    has_b = jnp.where(odd == 1, jnp.where(space < size - 1, 1, 0), jnp.where(space > 0, 1, 0))
    return blk % 2, odd, has_a, has_b, (blk // 2) % 2


def cost(micros):
    return pl.CostEstimate(flops=int(micros * 1e9), bytes_accessed=1, transcendentals=0)


def rows_of(chunks, start, count):
    for chunk in chunks:
        if start < chunk.shape[0]:
            return chunk[start:start + count, :]
        start -= chunk.shape[0]


def shape_of(rows, width):
    return jax.ShapeDtypeStruct((rows, width), F32)


def exchanged(value, axis, mask):
    count = lax.axis_size(axis)
    return lax.ppermute(value, axis, [(i, i ^ mask) for i in range(count)])


def halves(value):
    high = value.astype(BF16)
    return high, (value - high.astype(F32)).astype(BF16)


def gram(left, right):
    def one(a, b):
        return lax.dot_general(a, b, (((0,), (0,)), ((), ())), preferred_element_type=F32)

    left_high, left_low = halves(left)
    right_high, right_low = halves(right)
    return one(left_high, right_high) + (one(left_high, right_low) + one(left_low, right_high))


def thirds(value):
    high = value.astype(BF16)
    rest = value - high.astype(F32)
    middle = rest.astype(BF16)
    return high, middle, (rest - middle.astype(F32)).astype(BF16)


def product(left, right):
    a, b, c = thirds(left)
    x, y, z = thirds(right)

    def pair(one, two, three, four):
        return jnp.dot(
            jnp.concatenate([one, two], axis=1), jnp.concatenate([three, four], axis=0),
            preferred_element_type=F32,
        )

    return pair(a, a, x, y) + (pair(b, a, x, z) + pair(c, b, x, y))


def product_3(left, right):
    left_high, left_low = halves(left)
    right_high, right_low = halves(right)
    deep = jnp.dot(
        jnp.concatenate([left_high, left_low], axis=1),
        jnp.concatenate([right_high, right_high], axis=0),
        preferred_element_type=F32,
    )
    return deep + jnp.dot(left_high, right_low, preferred_element_type=F32)


def product_nt(left, right):
    def one(a, b):
        return lax.dot_general(a, b, (((1,), (1,)), ((), ())), preferred_element_type=F32)

    left_high, left_low = halves(left)
    right_high, right_low = halves(right)
    return one(left_high, right_high) + (one(left_high, right_low) + one(left_low, right_high))


def inner_image(at, i, layers, cells_z):
    v = at(i)
    layer, width = v.shape
    place = lax.broadcasted_iota(jnp.int32, (layer, width), 0) % cells_z
    near = at(min(i + 1, layers - 1)) + at(max(i - 1, 0))
    near = near + jnp.concatenate([v[cells_z:], v[-cells_z:]], axis=0)
    near = near + jnp.concatenate([v[:cells_z], v[:-cells_z]], axis=0)
    near = near + jnp.where(place == cells_z - 1, v, pltpu.roll(v, layer - 1, 0))
    near = near + jnp.where(place == 0, v, pltpu.roll(v, 1, 0))
    return 7.0 * v - near


def inner_kernel(cells_y, cells_z, *refs):
    layer = cells_y * cells_z
    chunks = refs[:CHUNKS]
    p_ref, w_ref, c_ref, d_ref = refs[CHUNKS:]
    layers = p_ref.shape[0] // layer
    width = p_ref.shape[1]
    high = place()[0] == 1
    cross = jnp.zeros((width, width), F32)
    diag = jnp.zeros((8, width), F32)

    def at(j):
        return rows_of(chunks, j * layer, layer)

    for i in range(layers):
        rows = slice(i * layer, (i + 1) * layer)
        v = at(i)
        image = inner_image(at, i, layers, cells_z)
        w_ref[rows, :] = image
        diag += jnp.sum((image * v).reshape(layer // 8, 8, width), axis=0)
        peer = p_ref[rows, :]
        cross += gram(jnp.where(high, peer, image), jnp.where(high, image, peer))
    c_ref[...] = cross
    d_ref[...] = diag


def edge_kernel(edge_a, edge_b, p_ref, c_ref, d_ref, near_a, near_b, step_ref, msg_ref):
    layer, width = edge_a.shape
    layers = p_ref.shape[0] // layer
    half = width // 2
    high = place()[0] == 1
    odd = place()[1]
    total = c_ref[...]
    diag = d_ref[...]
    for k, (spot, edge, halo, there) in enumerate((
        ((1 - odd) * (layers - 1), edge_a, near_a, place()[2]),
        (odd * (layers - 1), edge_b, near_b, place()[3]),
    )):
        rows = pl.ds(pl.multiple_of(spot * layer, layer), layer)
        v = edge[...]
        step = jnp.where(there == 1, v - halo[...], 0.0)
        step_ref[k * layer:(k + 1) * layer, :] = step
        diag = diag + jnp.sum((step * v).reshape(layer // 8, 8, width), axis=0)
        peer = p_ref[rows, :]
        total = total + gram(jnp.where(high, peer, step), jnp.where(high, step, peer))
    msg_ref[:half, :] = jnp.where(high, total[half:], total[:half])
    msg_ref[half:, :] = jnp.broadcast_to(jnp.sum(diag, axis=0, keepdims=True), (8, width))


def beside(value):
    return jnp.concatenate(halves(value), axis=1)


def down_product(high, low, right):
    width = right.shape[1]
    both = beside(right)
    total = jnp.dot(high, both, preferred_element_type=F32)
    return total[:, :width] + (
        total[:, width:] + jnp.dot(low, both[:, :width], preferred_element_type=F32)
    )


def near_kernel(layer, cells_z, wo, own_step, peer_step, *refs):
    chunks = refs[:CHUNKS]
    xp, out, high_t, low_t, wp = refs[CHUNKS:]
    width = xp.shape[1]
    layers = xp.shape[0] // layer
    odd = place()[1]

    def at(j):
        return xp[j * layer:(j + 1) * layer, :]

    for i in range(layers):
        wp[i * layer:(i + 1) * layer, :] = inner_image(at, i, layers, cells_z)
    for k, spot in enumerate(((1 - odd) * (layers - 1), odd * (layers - 1))):
        rows = pl.ds(pl.multiple_of(spot * layer, layer), layer)
        wp[rows, :] += peer_step[k * layer:(k + 1) * layer, :]
    for i in range(layers):
        rows = slice(i * layer, (i + 1) * layer)
        image = wo[rows, :]
        for k in range(2):
            if i in (0, layers - 1):
                here = ((1 - odd), odd)[k] * (layers - 1) == i
                image = image + jnp.where(here, own_step[k * layer:(k + 1) * layer, :], 0.0)
        left = jnp.concatenate([image.T, wp[rows, :].T], axis=0)
        high_t[:, rows], low_t[:, rows] = halves(left)
    own = jnp.concatenate([chunk[...] for chunk in chunks], axis=0)
    for k, value in enumerate((own, xp[...])):
        out[:, k * width:(k + 1) * width] = down_product(high_t[...], low_t[...], value)


def far_kernel(high_t, low_t, far_own, out):
    out[...] = down_product(high_t[...], low_t[...], far_own[...])


def edges_kernel(x_ref, edge_a, edge_b, sems):
    layer = edge_a.shape[0]
    last = x_ref.shape[0] - layer
    odd = place()[1]
    copies = [
        pltpu.make_async_copy(x_ref.at[pl.ds(pl.multiple_of(start, layer), layer)], out, sems.at[k])
        for k, (start, out) in enumerate((((1 - odd) * last, edge_a), (odd * last, edge_b)))
    ]
    for copy in copies:
        copy.start()
    for copy in copies:
        copy.wait()


def eye_of(width):
    row = lax.broadcasted_iota(jnp.int32, (width, width), 0)
    col = lax.broadcasted_iota(jnp.int32, (width, width), 1)
    return jnp.where(row == col, 1.0, 0.0).astype(F32)


def rotations(pairs, high, x_ref, finish):
    width = pairs[0][0].shape[1]
    half = width // 2
    eye = eye_of(width)
    sign = jnp.where(high, 2.0, -2.0)
    ratios, normals = [], []
    for own, other in pairs:
        cross = jnp.concatenate(
            [jnp.where(high, other[:half], own[:half]), jnp.where(high, own[:half], other[:half])], axis=0
        )
        cross_t = cross.T
        own_diag, other_diag = own[half:half + 1], other[half:half + 1]
        own_rows = jnp.broadcast_to(own_diag, (width, width)).T
        other_rows = jnp.broadcast_to(other_diag, (width, width)).T
        ratio = jnp.where(high, cross_t, cross) / (own_rows + other_diag)
        ratio_t = jnp.where(high, cross, cross_t) / (other_rows + own_diag)
        ratios.append(ratio)
        normals.append(eye + product(ratio, ratio_t))
    bound = jnp.max(jnp.sum(jnp.abs(normals[0]), axis=0, keepdims=True), axis=1, keepdims=True)
    for normal in normals[1:]:
        size = jnp.max(jnp.sum(jnp.abs(normal), axis=0, keepdims=True), axis=1, keepdims=True)
        bound = jnp.maximum(bound, size)
    scale = 2.0 / (bound + 1.0)
    err = (bound - 1.0) * (0.5 * scale)

    def next_of(err):
        fresh = 2.0 / (2.0 - err * err)
        return err * err * (0.5 * fresh), fresh

    err, fresh = next_of(err)
    boths = []
    for normal in normals:
        image = scale * normal
        turn = fresh * (2.0 * eye - image)
        boths.append(jnp.concatenate([scale * turn, product_3(turn, image)], axis=1))
    for _ in range(STEPS - 1):
        err, fresh = next_of(err)
        boths = [product_3(fresh * (2.0 * eye - both[:, width:]), both) for both in boths]

    def refined(inverses):
        size = 0.0
        turns = []
        for k, (inverse, ratio, normal) in enumerate(zip(inverses, ratios, normals)):
            left_over = eye - product(inverse, normal)
            both = jnp.concatenate([inverse, product(inverse, ratio)], axis=1)
            both = both + product_3(left_over, both)
            x_ref[k] = both[:, :width]
            turns.append((2.0 * both[:, :width] - eye, sign * both[:, width:]))
            size = jnp.maximum(size, jnp.max(jnp.sum(jnp.abs(left_over), axis=0)))
        finish(turns)
        return size

    size = refined([both[:, :width] for both in boths])
    lax.while_loop(
        lambda carry: (carry[0] > CLOSE) & (carry[1] < MORE),
        lambda carry: (refined([x_ref[k] for k in range(len(pairs))]), carry[1] + 1),
        (size, jnp.int32(0)),
    )


def first_kernel(far_msg, y_msg, core_msg, own_msg, own_t, far_t, x_ref):
    width = own_msg.shape[1]

    def finish(turns):
        for (keep, take), out in zip(turns, (own_t, far_t)):
            out[:, :width] = keep
            out[:, width:] = take

    pairs = [(own_msg[...], core_msg[...]), (y_msg[...], far_msg[...])]
    rotations(pairs, place()[0] == 1, x_ref, finish)


def apply_kernel(near_ref, far_ref, far_peer_ref, own_t, far_t, msg_ref):
    width = far_ref.shape[1]
    half = width // 2
    y_high = place()[4] == 1
    turn, far_turn = own_t[...], far_t[...]
    far_peer = jnp.concatenate([far_peer_ref[width:, :], far_peer_ref[:width, :]], axis=0)
    part = product_3(turn, jnp.concatenate([near_ref[...], far_ref[...], far_peer], axis=1))
    inside = turn * part[:, :2 * width]
    inside_high, inside_low = halves(inside)
    ones = jnp.ones((16, 2 * width), BF16)

    def lanes(value):
        return lax.dot_general(ones, value, (((1,), (1,)), ((), ())), preferred_element_type=F32)

    diag = lanes(inside_high) + lanes(inside_low)
    part = part[:, 2 * width:]
    cross = product_nt(jnp.where(y_high, far_turn, part), jnp.where(y_high, part, far_turn))
    msg_ref[:half, :] = jnp.where(y_high, cross[half:], cross[:half])
    msg_ref[half:, :] = diag[:8]


def wide_product(high_part, low_part, m_ref):
    width = m_ref.shape[1] // 2
    both = jnp.dot(high_part, m_ref[...], preferred_element_type=F32)
    rest = jnp.dot(low_part, m_ref[:, :width], preferred_element_type=F32)
    return both[:, :width] + (both[:, width:] + rest)


def turn_kernel(*refs):
    chunks = refs[:CHUNKS]
    xp, far_own, far_peer, own_t, far_t, high_ref, low_ref, m_ref = refs[CHUNKS:]
    width = xp.shape[1]
    step = 256
    for k, turn in enumerate((own_t, far_t)):
        m_ref[k, :, :width], m_ref[k, :, width:] = halves(
            jnp.concatenate([turn[:, :width].T, turn[:, width:].T], axis=0)
        )

    for i in range(xp.shape[0] // step):
        rows = slice(i * step, (i + 1) * step)
        ones = (rows_of(chunks, i * step, step), far_own[rows, :])
        for k, (one, two) in enumerate(zip(ones, (xp, far_peer))):
            parts = halves(jnp.concatenate([one, two[rows, :]], axis=1))
            turned = wide_product(*parts, m_ref.at[k])
            columns = slice(k * width, (k + 1) * width)
            high_ref[rows, columns], low_ref[rows, columns] = halves(turned)


def last_kernel(own_msg, y_msg, high_ref, low_ref, out, x_ref, m_ref, o_ref, sems):
    width = own_msg.shape[1]
    step = o_ref.shape[1]

    def finish(turns):
        keep, take = turns[0]
        m_ref[:, :width], m_ref[:, width:] = halves(jnp.concatenate([keep, take.T], axis=0))
        copies = []
        for k in range(o_ref.shape[0]):
            rows = slice(k * step, (k + 1) * step)
            o_ref[k] = wide_product(high_ref[rows, :], low_ref[rows, :], m_ref)
            copies.append(pltpu.make_async_copy(o_ref.at[k], out.at[pl.ds(k * step, step)], sems.at[k]))
            copies[-1].start()
        for copy in copies:
            copy.wait()

    rotations([(own_msg[...], y_msg[...])], place()[4] == 1, x_ref, finish)


def power_of_two(count):
    return count & (count - 1) == 0


def stages_of(count):
    bits = [1 << bit for bit in range(count.bit_length() - 1)]
    pairs = [tuple(bits[k:k + 2]) for k in range(0, len(bits) - 1, 2)]
    if len(bits) % 2 == 0:
        pairs[-1:] = [pairs[-1][:1]]
    return pairs + [(bits[-1],)]


def summed_over(value, stages):
    for bits in stages:
        if len(bits) == 1:
            value = value + exchanged(value, "space", bits[0])
        else:
            one, two = bits
            both, far, near = (exchanged(value, "space", mask) for mask in (one | two, two, one))
            value = (both + far) + (near + value)
    return value


def summed_over_space(value, beside_it):
    count = lax.axis_size("space")
    if not power_of_two(count):
        return lax.psum(value, "space")
    stages = stages_of(count)
    value = summed_over(value, stages[:-1])
    there = exchanged(value, "space", stages[-1][0])
    return lax.optimization_barrier((value, beside_it))[0] + there


def summed_with_y(value, beside_it):
    count, blocks = lax.axis_size("space"), lax.axis_size("blk")
    if not power_of_two(count):
        value = lax.psum(value, "space")
        return value, exchanged(value, "blk", 2)
    stages = stages_of(count)
    value = summed_over(value, stages[:-1])
    bit = stages[-1][0]
    route = [(i * blocks + j, (i ^ bit) * blocks + (j ^ 2)) for i in range(count) for j in range(blocks)]
    other_there = lax.ppermute(value, ("space", "blk"), route)
    there = exchanged(value, "space", bit)
    other = exchanged(value, "blk", 2)
    other_there, there, other = lax.optimization_barrier((other_there, there, other, beside_it))[:3]
    return value + there, other_there + other


def shards(snapshots):
    layers, cells_y, cells_z, width = snapshots.shape
    layer = cells_y * cells_z
    cells = layers * layer
    own = snapshots.reshape(cells, width)
    size = lax.axis_size("space")
    route_a = [(i, i ^ 1) for i in range(size) if i ^ 1 < size]
    route_b = [(i, j) for i in range(1, size - 1, 2) for j in (i + 1,)]
    route_b = route_b + [(j, i) for i, j in route_b]
    half_rows = width // 2 + 8

    def call(body, inputs, outputs, scratch, micros, name, **more):
        return pl.pallas_call(
            body,
            in_specs=[VMEM] * len(inputs),
            out_specs=[VMEM] * len(outputs),
            out_shape=outputs,
            scratch_shapes=scratch,
            compiler_params=PARAMS,
            cost_estimate=cost(micros),
            name=name,
            **more,
        )(*inputs)

    chunks = [own]
    peer = exchanged(own, "blk", 1)
    edge_a, edge_b = pl.pallas_call(
        edges_kernel,
        in_specs=[pl.BlockSpec(memory_space=pl.ANY)],
        out_specs=[VMEM] * 2,
        out_shape=[shape_of(layer, width)] * 2,
        scratch_shapes=[pltpu.SemaphoreType.DMA((2,))],
        compiler_params=pltpu.CompilerParams(vmem_limit_bytes=53 * 2**20),
        cost_estimate=cost(0.1),
        name="edges",
    )(own)
    near_a = lax.ppermute(edge_a, "space", route_a)
    near_b = lax.ppermute(edge_b, "space", route_b)
    far_own = exchanged(own, "blk", 2)

    image, cross, diag = call(
        lambda *refs: inner_kernel(cells_y, cells_z, *refs), [*chunks, peer],
        [shape_of(cells, width), shape_of(width, width), shape_of(8, width)], [], 0.1, "inner_grams",
    )
    steps, msg = call(
        edge_kernel, [edge_a, edge_b, peer, cross, diag, near_a, near_b],
        [shape_of(2 * layer, width), shape_of(half_rows, width)], [], 0.1, "edge_grams",
    )
    peer_steps = exchanged(steps, "blk", 1)
    turned_down = jax.ShapeDtypeStruct((2 * width, cells), BF16)
    near_grams, high_t, low_t = call(
        functools.partial(near_kernel, layer, cells_z), [image, steps, peer_steps, *chunks, peer],
        [shape_of(2 * width, 2 * width), turned_down, turned_down], [pltpu.VMEM((cells, width), F32)],
        2.5, "near_grams",
    )
    msg = summed_over_space(msg, near_grams)
    far_msg, y_msg, core_msg = (exchanged(msg, "blk", mask) for mask in (3, 2, 1))
    (far_grams,) = call(
        far_kernel, [high_t, low_t, far_own], [shape_of(2 * width, width)], [], 0.7, "far_grams"
    )
    far_peer_grams = exchanged(far_grams, "blk", 1)
    msg, far_grams = lax.optimization_barrier((msg, far_grams))
    own_t, far_t = call(
        first_kernel, [far_msg, y_msg, core_msg, msg], [shape_of(width, 2 * width)] * 2,
        [pltpu.VMEM((2, width, width), F32)], 4, "first_rotation",
    )
    (msg,) = call(
        apply_kernel, [near_grams, far_grams, far_peer_grams, own_t, far_t],
        [shape_of(half_rows, width)], [], 1.2, "rotated_grams",
    )
    far_own = lax.optimization_barrier((far_own, msg))[0]
    far_peer = exchanged(far_own, "blk", 1)
    bits = jax.ShapeDtypeStruct((cells, 2 * width), BF16)
    highs, lows = call(
        turn_kernel, [*chunks, peer, far_own, far_peer, own_t, far_t], [bits, bits],
        [pltpu.VMEM((2, 2 * width, 2 * width), BF16)], 1.4, "turned_blocks",
    )
    own_msg, y_msg = summed_with_y(msg, highs)

    step = 512
    mixed = pl.pallas_call(
        last_kernel,
        in_specs=[VMEM] * 4,
        out_specs=pl.BlockSpec(memory_space=pl.ANY),
        out_shape=shape_of(cells, width),
        scratch_shapes=[
            pltpu.VMEM((1, width, width), F32),
            pltpu.VMEM((2 * width, 2 * width), BF16),
            pltpu.VMEM((cells // step, step, width), F32),
            pltpu.SemaphoreType.DMA((cells // step,)),
        ],
        compiler_params=PARAMS,
        cost_estimate=cost(4),
        name="last_rotation",
    )(own_msg, y_msg, highs, lows)
    return mixed.reshape(snapshots.shape)


def solution(mesh):
    return jax.shard_map(
        shards,
        mesh=mesh,
        in_specs=(P("space", None, None, "blk"),),
        out_specs=P("space", None, None, "blk"),
        check_vma=False,
    )
```

```python
import functools

import jax
import jax.numpy as jnp
from jax import lax
from jax.experimental import pallas as pl
from jax.experimental.pallas import tpu as pltpu
from jax.sharding import PartitionSpec as P

F32 = jnp.float32
BF16 = jnp.bfloat16
VMEM = pl.BlockSpec(memory_space=pltpu.VMEM)
PARAMS = pltpu.CompilerParams(vmem_limit_bytes=40 * 2**20)
CLOSE = 2e-3
STEPS = 5
MORE = 8
CHUNKS = 1


def place():
    space = lax.axis_index("space")
    size = lax.axis_size("space")
    blk = lax.axis_index("blk")
    odd = space % 2
    has_a = jnp.where(odd == 1, 1, jnp.where(space < size - 1, 1, 0))
    has_b = jnp.where(odd == 1, jnp.where(space < size - 1, 1, 0), jnp.where(space > 0, 1, 0))
    return blk % 2, odd, has_a, has_b, (blk // 2) % 2


def cost(micros):
    return pl.CostEstimate(flops=int(micros * 1e9), bytes_accessed=1, transcendentals=0)


def rows_of(chunks, start, count):
    for chunk in chunks:
        if start < chunk.shape[0]:
            return chunk[start:start + count, :]
        start -= chunk.shape[0]


def shape_of(rows, width):
    return jax.ShapeDtypeStruct((rows, width), F32)


def exchanged(value, axis, mask):
    count = lax.axis_size(axis)
    return lax.ppermute(value, axis, [(i, i ^ mask) for i in range(count)])


def halves(value):
    high = value.astype(BF16)
    return high, (value - high.astype(F32)).astype(BF16)


def gram(left, right):
    def one(a, b):
        return lax.dot_general(a, b, (((0,), (0,)), ((), ())), preferred_element_type=F32)

    left_high, left_low = halves(left)
    right_high, right_low = halves(right)
    return one(left_high, right_high) + (one(left_high, right_low) + one(left_low, right_high))


def thirds(value):
    high = value.astype(BF16)
    rest = value - high.astype(F32)
    middle = rest.astype(BF16)
    return high, middle, (rest - middle.astype(F32)).astype(BF16)


def product(left, right):
    a, b, c = thirds(left)
    x, y, z = thirds(right)

    def pair(one, two, three, four):
        return jnp.dot(
            jnp.concatenate([one, two], axis=1), jnp.concatenate([three, four], axis=0),
            preferred_element_type=F32,
        )

    return pair(a, a, x, y) + (pair(b, a, x, z) + pair(c, b, x, y))


def product_3(left, right):
    left_high, left_low = halves(left)
    right_high, right_low = halves(right)
    deep = jnp.dot(
        jnp.concatenate([left_high, left_low], axis=1),
        jnp.concatenate([right_high, right_high], axis=0),
        preferred_element_type=F32,
    )
    return deep + jnp.dot(left_high, right_low, preferred_element_type=F32)


def product_nt(left, right):
    def one(a, b):
        return lax.dot_general(a, b, (((1,), (1,)), ((), ())), preferred_element_type=F32)

    left_high, left_low = halves(left)
    right_high, right_low = halves(right)
    return one(left_high, right_high) + (one(left_high, right_low) + one(left_low, right_high))


def inner_image(at, i, layers, cells_z):
    v = at(i)
    layer, width = v.shape
    place = lax.broadcasted_iota(jnp.int32, (layer, width), 0) % cells_z
    near = at(min(i + 1, layers - 1)) + at(max(i - 1, 0))
    near = near + jnp.concatenate([v[cells_z:], v[-cells_z:]], axis=0)
    near = near + jnp.concatenate([v[:cells_z], v[:-cells_z]], axis=0)
    near = near + jnp.where(place == cells_z - 1, v, pltpu.roll(v, layer - 1, 0))
    near = near + jnp.where(place == 0, v, pltpu.roll(v, 1, 0))
    return 7.0 * v - near


def inner_kernel(cells_y, cells_z, *refs):
    layer = cells_y * cells_z
    chunks = refs[:CHUNKS]
    p_ref, w_ref, c_ref, d_ref = refs[CHUNKS:]
    layers = p_ref.shape[0] // layer
    width = p_ref.shape[1]
    high = place()[0] == 1
    cross = jnp.zeros((width, width), F32)
    diag = jnp.zeros((8, width), F32)

    def at(j):
        return rows_of(chunks, j * layer, layer)

    for i in range(layers):
        rows = slice(i * layer, (i + 1) * layer)
        v = at(i)
        image = inner_image(at, i, layers, cells_z)
        w_ref[rows, :] = image
        diag += jnp.sum((image * v).reshape(layer // 8, 8, width), axis=0)
        peer = p_ref[rows, :]
        cross += gram(jnp.where(high, peer, image), jnp.where(high, image, peer))
    c_ref[...] = cross
    d_ref[...] = diag


def edge_kernel(edge_a, edge_b, p_ref, c_ref, d_ref, near_a, near_b, step_ref, msg_ref):
    layer, width = edge_a.shape
    layers = p_ref.shape[0] // layer
    half = width // 2
    high = place()[0] == 1
    odd = place()[1]
    total = c_ref[...]
    diag = d_ref[...]
    for k, (spot, edge, halo, there) in enumerate((
        ((1 - odd) * (layers - 1), edge_a, near_a, place()[2]),
        (odd * (layers - 1), edge_b, near_b, place()[3]),
    )):
        rows = pl.ds(pl.multiple_of(spot * layer, layer), layer)
        v = edge[...]
        step = jnp.where(there == 1, v - halo[...], 0.0)
        step_ref[k * layer:(k + 1) * layer, :] = step
        diag = diag + jnp.sum((step * v).reshape(layer // 8, 8, width), axis=0)
        peer = p_ref[rows, :]
        total = total + gram(jnp.where(high, peer, step), jnp.where(high, step, peer))
    msg_ref[:half, :] = jnp.where(high, total[half:], total[:half])
    msg_ref[half:, :] = jnp.broadcast_to(jnp.sum(diag, axis=0, keepdims=True), (8, width))


def beside(value):
    return jnp.concatenate(halves(value), axis=1)


def down_product(high, low, right):
    width = right.shape[1]
    both = beside(right)
    total = jnp.dot(high, both, preferred_element_type=F32)
    return total[:, :width] + (
        total[:, width:] + jnp.dot(low, both[:, :width], preferred_element_type=F32)
    )


def near_kernel(layer, cells_z, wo, own_step, peer_step, *refs):
    chunks = refs[:CHUNKS]
    xp, out, high_t, low_t, wp = refs[CHUNKS:]
    width = xp.shape[1]
    layers = xp.shape[0] // layer
    odd = place()[1]

    def at(j):
        return xp[j * layer:(j + 1) * layer, :]

    for i in range(layers):
        wp[i * layer:(i + 1) * layer, :] = inner_image(at, i, layers, cells_z)
    for k, spot in enumerate(((1 - odd) * (layers - 1), odd * (layers - 1))):
        rows = pl.ds(pl.multiple_of(spot * layer, layer), layer)
        wp[rows, :] += peer_step[k * layer:(k + 1) * layer, :]
    for i in range(layers):
        rows = slice(i * layer, (i + 1) * layer)
        image = wo[rows, :]
        for k in range(2):
            if i in (0, layers - 1):
                here = ((1 - odd), odd)[k] * (layers - 1) == i
                image = image + jnp.where(here, own_step[k * layer:(k + 1) * layer, :], 0.0)
        left = jnp.concatenate([image.T, wp[rows, :].T], axis=0)
        high_t[:, rows], low_t[:, rows] = halves(left)
    own = jnp.concatenate([chunk[...] for chunk in chunks], axis=0)
    for k, value in enumerate((own, xp[...])):
        out[:, k * width:(k + 1) * width] = down_product(high_t[...], low_t[...], value)


def far_kernel(high_t, low_t, far_own, out):
    out[...] = down_product(high_t[...], low_t[...], far_own[...])


def edges_kernel(x_ref, edge_a, edge_b, sems):
    layer = edge_a.shape[0]
    last = x_ref.shape[0] - layer
    odd = place()[1]
    copies = [
        pltpu.make_async_copy(x_ref.at[pl.ds(pl.multiple_of(start, layer), layer)], out, sems.at[k])
        for k, (start, out) in enumerate((((1 - odd) * last, edge_a), (odd * last, edge_b)))
    ]
    for copy in copies:
        copy.start()
    for copy in copies:
        copy.wait()


def eye_of(width):
    row = lax.broadcasted_iota(jnp.int32, (width, width), 0)
    col = lax.broadcasted_iota(jnp.int32, (width, width), 1)
    return jnp.where(row == col, 1.0, 0.0).astype(F32)


def rotations(pairs, high, x_ref, finish):
    width = pairs[0][0].shape[1]
    half = width // 2
    eye = eye_of(width)
    sign = jnp.where(high, 2.0, -2.0)
    ratios, normals = [], []
    for own, other in pairs:
        cross = jnp.concatenate(
            [jnp.where(high, other[:half], own[:half]), jnp.where(high, own[:half], other[:half])], axis=0
        )
        cross_t = cross.T
        own_diag, other_diag = own[half:half + 1], other[half:half + 1]
        own_rows = jnp.broadcast_to(own_diag, (width, width)).T
        other_rows = jnp.broadcast_to(other_diag, (width, width)).T
        ratio = jnp.where(high, cross_t, cross) / (own_rows + other_diag)
        ratio_t = jnp.where(high, cross, cross_t) / (other_rows + own_diag)
        ratios.append(ratio)
        normals.append(eye + product(ratio, ratio_t))
    bound = jnp.max(jnp.sum(jnp.abs(normals[0]), axis=0, keepdims=True), axis=1, keepdims=True)
    for normal in normals[1:]:
        size = jnp.max(jnp.sum(jnp.abs(normal), axis=0, keepdims=True), axis=1, keepdims=True)
        bound = jnp.maximum(bound, size)
    scale = 2.0 / (bound + 1.0)
    err = (bound - 1.0) * (0.5 * scale)

    def next_of(err):
        fresh = 2.0 / (2.0 - err * err)
        return err * err * (0.5 * fresh), fresh

    err, fresh = next_of(err)
    boths = []
    for normal in normals:
        image = scale * normal
        turn = fresh * (2.0 * eye - image)
        boths.append(jnp.concatenate([scale * turn, product_3(turn, image)], axis=1))
    for _ in range(STEPS - 1):
        err, fresh = next_of(err)
        boths = [product_3(fresh * (2.0 * eye - both[:, width:]), both) for both in boths]

    def refined(inverses):
        size = 0.0
        turns = []
        for k, (inverse, ratio, normal) in enumerate(zip(inverses, ratios, normals)):
            left_over = eye - product(inverse, normal)
            both = jnp.concatenate([inverse, product(inverse, ratio)], axis=1)
            both = both + product_3(left_over, both)
            x_ref[k] = both[:, :width]
            turns.append((2.0 * both[:, :width] - eye, sign * both[:, width:]))
            size = jnp.maximum(size, jnp.max(jnp.sum(jnp.abs(left_over), axis=0)))
        finish(turns)
        return size

    size = refined([both[:, :width] for both in boths])
    lax.while_loop(
        lambda carry: (carry[0] > CLOSE) & (carry[1] < MORE),
        lambda carry: (refined([x_ref[k] for k in range(len(pairs))]), carry[1] + 1),
        (size, jnp.int32(0)),
    )


def first_kernel(far_msg, y_msg, core_msg, own_msg, own_t, far_t, x_ref):
    width = own_msg.shape[1]

    def finish(turns):
        for (keep, take), out in zip(turns, (own_t, far_t)):
            out[:, :width] = keep
            out[:, width:] = take

    pairs = [(own_msg[...], core_msg[...]), (y_msg[...], far_msg[...])]
    rotations(pairs, place()[0] == 1, x_ref, finish)


def apply_kernel(near_ref, far_ref, far_peer_ref, own_t, far_t, msg_ref):
    width = far_ref.shape[1]
    half = width // 2
    y_high = place()[4] == 1
    turn, far_turn = own_t[...], far_t[...]
    far_peer = jnp.concatenate([far_peer_ref[width:, :], far_peer_ref[:width, :]], axis=0)
    part = product_3(turn, jnp.concatenate([near_ref[...], far_ref[...], far_peer], axis=1))
    inside = turn * part[:, :2 * width]
    inside_high, inside_low = halves(inside)
    ones = jnp.ones((16, 2 * width), BF16)

    def lanes(value):
        return lax.dot_general(ones, value, (((1,), (1,)), ((), ())), preferred_element_type=F32)

    diag = lanes(inside_high) + lanes(inside_low)
    part = part[:, 2 * width:]
    cross = product_nt(jnp.where(y_high, far_turn, part), jnp.where(y_high, part, far_turn))
    msg_ref[:half, :] = jnp.where(y_high, cross[half:], cross[:half])
    msg_ref[half:, :] = diag[:8]


def wide_product(high_part, low_part, m_ref):
    width = m_ref.shape[1] // 2
    both = jnp.dot(high_part, m_ref[...], preferred_element_type=F32)
    rest = jnp.dot(low_part, m_ref[:, :width], preferred_element_type=F32)
    return both[:, :width] + (both[:, width:] + rest)


def turn_kernel(*refs):
    chunks = refs[:CHUNKS]
    xp, far_own, far_peer, own_t, far_t, high_ref, low_ref, m_ref = refs[CHUNKS:]
    width = xp.shape[1]
    step = 256
    for k, turn in enumerate((own_t, far_t)):
        m_ref[k, :, :width], m_ref[k, :, width:] = halves(
            jnp.concatenate([turn[:, :width].T, turn[:, width:].T], axis=0)
        )

    for i in range(xp.shape[0] // step):
        rows = slice(i * step, (i + 1) * step)
        ones = (rows_of(chunks, i * step, step), far_own[rows, :])
        for k, (one, two) in enumerate(zip(ones, (xp, far_peer))):
            parts = halves(jnp.concatenate([one, two[rows, :]], axis=1))
            turned = wide_product(*parts, m_ref.at[k])
            columns = slice(k * width, (k + 1) * width)
            high_ref[rows, columns], low_ref[rows, columns] = halves(turned)


def last_kernel(own_msg, y_msg, high_ref, low_ref, out, x_ref, m_ref, o_ref, sems):
    width = own_msg.shape[1]
    step = o_ref.shape[1]

    def finish(turns):
        keep, take = turns[0]
        m_ref[:, :width], m_ref[:, width:] = halves(jnp.concatenate([keep, take.T], axis=0))
        copies = []
        for k in range(o_ref.shape[0]):
            rows = slice(k * step, (k + 1) * step)
            o_ref[k] = wide_product(high_ref[rows, :], low_ref[rows, :], m_ref)
            copies.append(pltpu.make_async_copy(o_ref.at[k], out.at[pl.ds(k * step, step)], sems.at[k]))
            copies[-1].start()
        for copy in copies:
            copy.wait()

    rotations([(own_msg[...], y_msg[...])], place()[4] == 1, x_ref, finish)


def power_of_two(count):
    return count & (count - 1) == 0


def stages_of(count):
    bits = [1 << bit for bit in range(count.bit_length() - 1)]
    pairs = [tuple(bits[k:k + 2]) for k in range(0, len(bits) - 1, 2)]
    if len(bits) % 2 == 0:
        pairs[-1:] = [pairs[-1][:1]]
    return pairs + [(bits[-1],)]


def summed_over(value, stages):
    for bits in stages:
        if len(bits) == 1:
            value = value + exchanged(value, "space", bits[0])
        else:
            one, two = bits
            both, far, near = (exchanged(value, "space", mask) for mask in (one | two, two, one))
            value = (both + far) + (near + value)
    return value


def summed_over_space(value, beside_it):
    count = lax.axis_size("space")
    if not power_of_two(count):
        return lax.psum(value, "space")
    stages = stages_of(count)
    value = summed_over(value, stages[:-1])
    there = exchanged(value, "space", stages[-1][0])
    return lax.optimization_barrier((value, beside_it))[0] + there


def summed_with_y(value, beside_it):
    count, blocks = lax.axis_size("space"), lax.axis_size("blk")
    if not power_of_two(count):
        value = lax.psum(value, "space")
        return value, exchanged(value, "blk", 2)
    stages = stages_of(count)
    value = summed_over(value, stages[:-1])
    bit = stages[-1][0]
    route = [(i * blocks + j, (i ^ bit) * blocks + (j ^ 2)) for i in range(count) for j in range(blocks)]
    other_there = lax.ppermute(value, ("space", "blk"), route)
    there = exchanged(value, "space", bit)
    other = exchanged(value, "blk", 2)
    other_there, there, other = lax.optimization_barrier((other_there, there, other, beside_it))[:3]
    return value + there, other_there + other


def shards(snapshots):
    layers, cells_y, cells_z, width = snapshots.shape
    layer = cells_y * cells_z
    cells = layers * layer
    own = snapshots.reshape(cells, width)
    size = lax.axis_size("space")
    route_a = [(i, i ^ 1) for i in range(size) if i ^ 1 < size]
    route_b = [(i, j) for i in range(1, size - 1, 2) for j in (i + 1,)]
    route_b = route_b + [(j, i) for i, j in route_b]
    half_rows = width // 2 + 8

    def call(body, inputs, outputs, scratch, micros, name, **more):
        return pl.pallas_call(
            body,
            in_specs=[VMEM] * len(inputs),
            out_specs=[VMEM] * len(outputs),
            out_shape=outputs,
            scratch_shapes=scratch,
            compiler_params=PARAMS,
            cost_estimate=cost(micros),
            name=name,
            **more,
        )(*inputs)

    chunks = [own]
    peer = exchanged(own, "blk", 1)
    edge_a, edge_b = pl.pallas_call(
        edges_kernel,
        in_specs=[pl.BlockSpec(memory_space=pl.ANY)],
        out_specs=[VMEM] * 2,
        out_shape=[shape_of(layer, width)] * 2,
        scratch_shapes=[pltpu.SemaphoreType.DMA((2,))],
        compiler_params=pltpu.CompilerParams(vmem_limit_bytes=53 * 2**20),
        cost_estimate=cost(0.1),
        name="edges",
    )(own)
    near_a = lax.ppermute(edge_a, "space", route_a)
    near_b = lax.ppermute(edge_b, "space", route_b)
    far_own = exchanged(own, "blk", 2)

    image, cross, diag = call(
        lambda *refs: inner_kernel(cells_y, cells_z, *refs), [*chunks, peer],
        [shape_of(cells, width), shape_of(width, width), shape_of(8, width)], [], 0.1, "inner_grams",
    )
    steps, msg = call(
        edge_kernel, [edge_a, edge_b, peer, cross, diag, near_a, near_b],
        [shape_of(2 * layer, width), shape_of(half_rows, width)], [], 0.1, "edge_grams",
    )
    peer_steps = exchanged(steps, "blk", 1)
    turned_down = jax.ShapeDtypeStruct((2 * width, cells), BF16)
    near_grams, high_t, low_t = call(
        functools.partial(near_kernel, layer, cells_z), [image, steps, peer_steps, *chunks, peer],
        [shape_of(2 * width, 2 * width), turned_down, turned_down], [pltpu.VMEM((cells, width), F32)],
        2.5, "near_grams",
    )
    msg = summed_over_space(msg, near_grams)
    far_msg, y_msg, core_msg = (exchanged(msg, "blk", mask) for mask in (3, 2, 1))
    (far_grams,) = call(
        far_kernel, [high_t, low_t, far_own], [shape_of(2 * width, width)], [], 0.7, "far_grams"
    )
    far_peer_grams = exchanged(far_grams, "blk", 1)
    msg, far_grams = lax.optimization_barrier((msg, far_grams))
    own_t, far_t = call(
        first_kernel, [far_msg, y_msg, core_msg, msg], [shape_of(width, 2 * width)] * 2,
        [pltpu.VMEM((2, width, width), F32)], 4, "first_rotation",
    )
    (msg,) = call(
        apply_kernel, [near_grams, far_grams, far_peer_grams, own_t, far_t],
        [shape_of(half_rows, width)], [], 1.2, "rotated_grams",
    )
    far_own = lax.optimization_barrier((far_own, msg))[0]
    far_peer = exchanged(far_own, "blk", 1)
    bits = jax.ShapeDtypeStruct((cells, 2 * width), BF16)
    highs, lows = call(
        turn_kernel, [*chunks, peer, far_own, far_peer, own_t, far_t], [bits, bits],
        [pltpu.VMEM((2, 2 * width, 2 * width), BF16)], 1.4, "turned_blocks",
    )
    own_msg, y_msg = summed_with_y(msg, highs)

    step = 256
    mixed = pl.pallas_call(
        last_kernel,
        in_specs=[VMEM] * 4,
        out_specs=pl.BlockSpec(memory_space=pl.ANY),
        out_shape=shape_of(cells, width),
        scratch_shapes=[
            pltpu.VMEM((1, width, width), F32),
            pltpu.VMEM((2 * width, 2 * width), BF16),
            pltpu.VMEM((cells // step, step, width), F32),
            pltpu.SemaphoreType.DMA((cells // step,)),
        ],
        compiler_params=PARAMS,
        cost_estimate=cost(4),
        name="last_rotation",
    )(own_msg, y_msg, highs, lows)
    return mixed.reshape(snapshots.shape)


def solution(mesh):
    return jax.shard_map(
        shards,
        mesh=mesh,
        in_specs=(P("space", None, None, "blk"),),
        out_specs=P("space", None, None, "blk"),
        check_vma=False,
    )
```
